512 devices in a mesh: grp: 32 (over x, z_lo, core), fsdp: 8 (over y), rep: 2 (over z_hi).
Axes of the slice: x: 4, y: 8, z: 8 (z_hi: 2, z_lo: 4; z = z_hi * 4 + z_lo), core: 2. Of those that a mesh axis runs over, the one named last changes fastest.
Arguments:
- grad_parts: bfloat16 [2, 4608, 4608], P('rep', 'grp', 'fsdp'), may hold values from -6 to 6
- basis_in: float32 [4608, 4608], P('grp', 'fsdp'), may hold values from -0.09375 to 0.09375
- basis_out: float32 [4608, 4608], P('grp', 'fsdp'), may hold values from -0.09375 to 0.09375
- eig_in: float32 [4608], replicated, may hold values from 0.3 to 3
- eig_out: float32 [4608], replicated, may hold values from 0.3 to 3
Outputs:
- preconditioned: bfloat16 [4608, 4608], P('grp', ('fsdp', 'rep'))
The draws below stay inside these ranges and needn't reach their ends.
All inputs are finite; a program needn't handle non-finite values.
Results may differ from the reference program's by a relative error of at most 0.03.
Values may be sent and summed in bfloat16 or wider, within the bound.
No kernel may reach another device: no remote copies, remote signals or barrier semaphores. Data moves between devices by JAX's collectives and lax.ppermute only.
A program may use at most 64 MiB of HBM per device.

```python
import math
import jax
import jax.numpy as jnp

WIDTH = 4608
REPLICAS = 2
ROT_BLOCKS = 16
ROW_BLOCKS = 32


def levels(key, dims, pieces, smallest, largest):
    gain, own = 1.0, jax.random.fold_in(key, 6)
    for position, blocks in pieces:
        heights = jnp.exp(jax.random.uniform(jax.random.fold_in(own, position), (blocks,), jnp.float32, smallest / len(pieces), largest / len(pieces)))
        gain = gain * jnp.repeat(heights, dims[position] // blocks).reshape([-1 if axis == position else 1 for axis in range(len(dims))])
    return gain


def normal_values(stream_key, shape, width, most, cuts=(), dtype=jnp.bfloat16):
    values = jax.random.normal(stream_key, shape, jnp.float32) * width
    if len(cuts) > 0:
        values = levels(stream_key, shape, cuts, -0.22, 0.18) * values
    return jnp.clip(values, min=-most, max=most).astype(dtype)


def setup_inputs(seed: int = 0) -> dict:
    seeds = jax.random.split(jax.random.key(seed), 6)
    return {
        "grad_parts": normal_values(seeds[0], (REPLICAS, WIDTH, WIDTH), 1.0, 6.0, ((0, 2), (1, 32), (2, 8))),
        "basis_in": normal_values(seeds[1], (WIDTH, WIDTH), WIDTH ** -0.5, 0.09375, ((0, 32), (1, 8)), jnp.float32),
        "basis_out": normal_values(seeds[2], (WIDTH, WIDTH), WIDTH ** -0.5, 0.09375, ((0, 32), (1, 8)), jnp.float32),
        "eig_in": jnp.clip(jnp.exp(jax.random.uniform(seeds[3], (WIDTH,), jnp.float32, math.log(0.3), math.log(3.0))), 0.3, 3.0),
        "eig_out": jnp.clip(jnp.exp(jax.random.uniform(seeds[4], (WIDTH,), jnp.float32, math.log(0.3), math.log(3.0))), 0.3, 3.0),
    }


DAMPING = 0.1


def reference(grad_parts, basis_in, basis_out, eig_in, eig_out):
    grad = jnp.sum(grad_parts.astype(jnp.float32), axis=0).astype(jnp.bfloat16)
    in_basis = basis_in.astype(jnp.bfloat16)
    out_rows = basis_out.astype(jnp.bfloat16)
    rotated_in = jnp.dot(grad, in_basis, preferred_element_type=jnp.float32).astype(jnp.bfloat16)
    rotated = jnp.dot(out_rows, rotated_in, preferred_element_type=jnp.float32)
    scaled = (rotated / (eig_out[:, None] * eig_in[None, :] + DAMPING)).astype(jnp.bfloat16)
    col_width = WIDTH // ROT_BLOCKS
    back_total = jnp.zeros((WIDTH, WIDTH), jnp.float32)
    for block in range(ROT_BLOCKS):
        left = scaled[:, block * col_width:(block + 1) * col_width]
        right = in_basis[:, block * col_width:(block + 1) * col_width]
        part = jnp.dot(left, right.T, preferred_element_type=jnp.float32).astype(jnp.bfloat16)
        back_total = back_total + part.astype(jnp.float32)
    back_in = back_total.astype(jnp.bfloat16)
    row_width = WIDTH // ROW_BLOCKS
    final_total = jnp.zeros((WIDTH, WIDTH), jnp.float32)
    for block in range(ROW_BLOCKS):
        left = out_rows[block * row_width:(block + 1) * row_width, :]
        right = back_in[block * row_width:(block + 1) * row_width, :]
        part = jnp.dot(left.T, right, preferred_element_type=jnp.float32).astype(jnp.bfloat16)
        final_total = final_total + part.astype(jnp.float32)
    return final_total.astype(jnp.bfloat16)
```

```python
import jax
import jax.numpy as jnp
from jax import lax
from jax.sharding import Mesh, PartitionSpec as P

DAMPING = 0.1
AXES = ("x", "z1", "z0", "c", "y", "z2")
ROWS = ("x", "z1", "z0", "c")
RING = ("x", "z0")
PART = ("z1", "z2")


def gather(block, axes, count):
    return lax.all_to_all(
        jnp.broadcast_to(block[None], (count,) + block.shape), axes, 0, 0, tiled=True
    )


def scatter_sum(blocks, axes):
    got = lax.all_to_all(blocks, axes, 0, 0, tiled=True)
    return jnp.sum(got.astype(jnp.float32), axis=0)


def pack(rows):
    q = rows.shape[0] // 4
    return jnp.concatenate([rows[i * q : (i + 1) * q] for i in range(4)], axis=1)


def dot(left, right, left_dim, right_dim):
    return lax.dot_general(
        left, right, (((left_dim,), (right_dim,)), ((), ())), preferred_element_type=jnp.float32
    )


def pairs_z1z0_cz2():
    out = []
    for z1 in range(2):
        for z0 in range(2):
            for c in range(2):
                for z2 in range(2):
                    out.append((z1 * 8 + z0 * 4 + c * 2 + z2, z0 * 8 + z1 * 4 + z2 * 2 + c))
    return out


def pairs_z1y0():
    out = []
    for z1 in range(2):
        for y in range(8):
            out.append((z1 * 8 + y, (y % 2) * 8 + (y // 2) * 2 + z1))
    return out


SWAP = [(0, 1), (1, 0)]


def body(grad_parts, basis_in, basis_out, eig_in, eig_out):
    bf16, f32 = jnp.bfloat16, jnp.float32
    x, z1, z0, c, y, z2 = (lax.axis_index(a) for a in AXES)
    rows, cols = basis_in.shape
    half, quarter = rows // 2, cols // 4
    wide = 2 * rows

    bi = basis_in.astype(bf16)
    bi = jnp.where(z2 == 0, bi[:half], bi[half:])
    bi = lax.ppermute(bi, ("z1", "z0", "c", "z2"), pairs_z1z0_cz2())
    bi = gather(bi, RING, 8)
    bi_other = lax.ppermute(bi, "c", SWAP)
    bi = jnp.where(
        c == 0, jnp.concatenate([bi, bi_other], axis=1), jnp.concatenate([bi_other, bi], axis=1)
    ).reshape(8 * rows, cols)

    bo = basis_out.astype(bf16)
    lo = jnp.concatenate([bo[:, i * quarter : i * quarter + half] for i in range(4)], axis=1)
    hi = jnp.concatenate([bo[:, i * quarter + half : (i + 1) * quarter] for i in range(4)], axis=1)
    bo = jnp.where(z2 == 0, lo, hi)
    bo = jnp.concatenate([bo[:half], bo[half:]], axis=1)
    bo = lax.ppermute(bo, ("z1", "y"), pairs_z1y0())
    bo = gather(bo, "y", 8)
    bo = bo.reshape(4, 2, half, 2, wide).transpose(1, 3, 2, 0, 4).reshape(wide, 4 * wide)

    grad = grad_parts[0]
    parts = jnp.stack([grad[:, i * quarter : (i + 1) * quarter] for i in range(4)])
    got = lax.all_to_all(parts, PART, 0, 0, tiled=True).astype(f32)
    got = got.reshape(2, 2, rows, quarter)
    grad = (got[:, 0] + got[:, 1]).astype(bf16).reshape(wide, quarter)
    grad = gather(pack(grad), "y", 8)
    grad = grad.reshape(8, half, 4, quarter).transpose(2, 1, 0, 3).reshape(wide, 8 * quarter)

    part = dot(grad, bi, 1, 0).astype(bf16).reshape(4, half, cols)
    turned = scatter_sum(part, PART).astype(bf16)
    turned = gather(turned, RING, 8)
    other = lax.ppermute(turned, "c", SWAP)
    turned = jnp.where(
        c == 0, jnp.stack([turned, other], axis=1), jnp.stack([other, turned], axis=1)
    ).reshape(16 * half, cols)

    part = dot(bo, turned, 1, 0).astype(bf16).reshape(4, half, cols)
    rotated = scatter_sum(part, PART)
    first = (((x * 2 + z1) * 2 + z0) * 2 + c) * rows + z2 * half
    out_scale = lax.dynamic_slice_in_dim(eig_out, first, half, 0)
    in_scale = lax.dynamic_slice_in_dim(eig_in, y * cols, cols, 0)
    scaled = (rotated / (out_scale[:, None] * in_scale[None, :] + DAMPING)).astype(bf16)
    scaled = gather(scaled, PART, 4).reshape(wide, cols)

    part = dot(scaled, bi, 1, 1).astype(bf16)
    part = part.reshape(4, half, 8, quarter).transpose(2, 1, 0, 3).reshape(8, half, cols)
    back = scatter_sum(part, "y").astype(bf16)
    back = gather(back, PART, 4)
    back = back.reshape(4, half, 4, quarter).transpose(2, 1, 0, 3).reshape(wide, cols)

    part = dot(bo, back, 0, 0).reshape(8, 2, half, cols)
    keep = jnp.where(c == 0, part[:, 0], part[:, 1])
    give = jnp.where(c == 0, part[:, 1], part[:, 0]).astype(bf16)
    part = (keep + lax.ppermute(give, "c", SWAP).astype(f32)).astype(bf16)
    out = scatter_sum(part, RING).astype(bf16)

    keep = jnp.where(z2 == 0, out[:, : cols // 2], out[:, cols // 2 :])
    give = jnp.where(z2 == 0, out[:, cols // 2 :], out[:, : cols // 2])
    other = lax.ppermute(give, "z2", SWAP)
    return jnp.where(
        z2 == 0, jnp.concatenate([keep, other], axis=0), jnp.concatenate([other, keep], axis=0)
    )


def solution(mesh):
    fine = Mesh(mesh.devices.reshape(4, 2, 2, 2, 8, 2), AXES)
    in_specs = (P("z2", ROWS, "y"), P(ROWS, "y"), P(ROWS, "y"), P(), P())
    out_specs = P(ROWS, ("y", "z2"))
    return jax.shard_map(body, mesh=fine, in_specs=in_specs, out_specs=out_specs, check_vma=False)
```

```python
import jax
import jax.numpy as jnp
from jax import lax
from jax.sharding import Mesh, PartitionSpec as P

DAMPING = 0.1
AXES = ("x", "z1", "z0", "c", "y", "z2")
ROWS = ("x", "z1", "z0", "c")
RING = ("x", "z0")
PART = ("z1", "z2")
SWAP = [(0, 1), (1, 0)]


def gather(block, axes, count):
    return lax.all_to_all(
        jnp.broadcast_to(block[None], (count,) + block.shape), axes, 0, 0, tiled=True
    )


def scatter_sum(blocks, axes):
    got = lax.all_to_all(blocks, axes, 0, 0, tiled=True)
    return jnp.sum(got.astype(jnp.float32), axis=0)


def dot(left, right, left_dim, right_dim):
    return lax.dot_general(
        left, right, (((left_dim,), (right_dim,)), ((), ())), preferred_element_type=jnp.float32
    )


def in_order(first, mine, other, axis):
    return jnp.where(
        first,
        jnp.concatenate([mine, other], axis=axis),
        jnp.concatenate([other, mine], axis=axis),
    )


def pairs_z1y0():
    return [(z1 * 8 + y, (y % 2) * 8 + (y // 2) * 2 + z1) for z1 in range(2) for y in range(8)]


def body(grad_parts, basis_in, basis_out, eig_in, eig_out):
    bf16, f32 = jnp.bfloat16, jnp.float32
    x, z1, z0, c, y, z2 = (lax.axis_index(a) for a in AXES)
    rows, cols = basis_in.shape
    half, quarter = rows // 2, cols // 4
    wide = 2 * rows
    low_core, low_rep = c == 0, z2 == 0

    bi = lax.all_gather(basis_in.astype(bf16), ("x", "z1", "z0"), axis=0, tiled=True)

    bo = lax.ppermute(basis_out.astype(bf16), ("z1", "y"), pairs_z1y0())
    bo = lax.all_gather(bo, ("c", "y"), axis=0, tiled=True).reshape(2, 4, 2, rows, cols)

    grad = grad_parts[0]
    keep = jnp.where(low_rep, grad[:half], grad[half:])
    give = jnp.where(low_rep, grad[half:], grad[:half])
    got = lax.ppermute(give, "z2", SWAP)
    grad = (keep.astype(f32) + got.astype(f32)).astype(bf16)
    even = jnp.concatenate([grad[:, :quarter], grad[:, 2 * quarter : 3 * quarter]], axis=1)
    odd = jnp.concatenate([grad[:, quarter : 2 * quarter], grad[:, 3 * quarter :]], axis=1)
    keep, give = jnp.where(low_core, even, odd), jnp.where(low_core, odd, even)
    grad = in_order(low_core, keep, lax.ppermute(give, "c", SWAP), 1)
    grad = gather(grad, "y", 8)
    grad = grad.reshape(8, half, 2, wide).transpose(2, 1, 0, 3).reshape(rows, 8 * wide)

    part = dot(grad, bi, 1, 0)
    keep = jnp.where(low_core, part[:half], part[half:])
    give = jnp.where(low_core, part[half:], part[:half]).astype(bf16)
    turned = (keep + lax.ppermute(give, "c", SWAP).astype(f32)).astype(bf16)
    turned = gather(turned, RING, 8)
    other = lax.ppermute(turned, "c", SWAP)
    turned = in_order(low_core, turned[:, None], other[:, None], 1).reshape(16 * half, cols)

    mine = lax.dynamic_index_in_dim(bo, c, 0, keepdims=False).reshape(4, wide, 4, 2, half)
    mine = lax.dynamic_index_in_dim(mine, z2, 3, keepdims=False)
    mine = mine.transpose(1, 0, 2, 3).reshape(wide, 4 * wide)
    part = dot(mine, turned, 1, 0).astype(bf16).reshape(4, half, cols)
    rotated = scatter_sum(part, PART)
    first = (((x * 2 + z1) * 2 + z0) * 2 + c) * rows + z2 * half
    out_scale = lax.dynamic_slice_in_dim(eig_out, first, half, 0)
    in_scale = lax.dynamic_slice_in_dim(eig_in, y * cols, cols, 0)
    scaled = (rotated / (out_scale[:, None] * in_scale[None, :] + DAMPING)).astype(bf16)
    scaled = in_order(low_core, scaled, lax.ppermute(scaled, "c", SWAP), 0)

    part = dot(scaled, bi, 1, 1).astype(bf16)
    part = part.reshape(2, half, 8, wide).transpose(2, 1, 0, 3).reshape(8, half, cols)
    back = scatter_sum(part, "y").astype(bf16)
    low = jnp.concatenate([back[:, :quarter], back[:, 2 * quarter : 3 * quarter]], axis=1)
    high = jnp.concatenate([back[:, quarter : 2 * quarter], back[:, 3 * quarter :]], axis=1)
    back = lax.all_to_all(jnp.stack([low, high, low, high]), PART, 0, 0, tiled=True)
    back = back.reshape(4 * half, 2, quarter).transpose(1, 0, 2).reshape(8 * half, quarter)

    left = bo.transpose(0, 2, 3, 1, 4).reshape(8 * half, 4 * cols)
    part = dot(left, back, 0, 0).astype(bf16).reshape(8, 4, half, quarter)
    part = part.transpose(0, 2, 1, 3).reshape(8, half, cols)
    out = scatter_sum(part, RING).astype(bf16)
    keep = jnp.where(low_core, out[:, :wide], out[:, wide:])
    give = jnp.where(low_core, out[:, wide:], out[:, :wide])
    got = lax.ppermute(give, "c", SWAP)
    mine = jnp.concatenate([keep[:, :quarter], keep[:, quarter:]], axis=0)
    got = jnp.concatenate([got[:, :quarter], got[:, quarter:]], axis=0)
    return in_order(low_core, mine, got, 1)


def solution(mesh):
    fine = Mesh(mesh.devices.reshape(4, 2, 2, 2, 8, 2), AXES)
    in_specs = (P("z2", ROWS, "y"), P(ROWS, "y"), P(ROWS, "y"), P(), P())
    out_specs = P(ROWS, ("y", "z2"))
    return jax.shard_map(body, mesh=fine, in_specs=in_specs, out_specs=out_specs, check_vma=False)
```

```python
import jax
import jax.numpy as jnp
from jax import lax
from jax.sharding import Mesh, PartitionSpec as P

DAMPING = 0.1
AXES = ("x", "z1", "z0", "c", "y", "z2")
ROWS = ("x", "z1", "z0", "c")
RING = ("x", "z0")
PART = ("z1", "z2")
SWAP = [(0, 1), (1, 0)]


def gather(block, axes, count):
    return lax.all_to_all(
        jnp.broadcast_to(block[None], (count,) + block.shape), axes, 0, 0, tiled=True
    )


def scatter_sum(blocks, axes):
    got = lax.all_to_all(blocks, axes, 0, 0, tiled=True)
    return jnp.sum(got.astype(jnp.float32), axis=0)


def dot(left, right, left_dim, right_dim):
    return lax.dot_general(
        left, right, (((left_dim,), (right_dim,)), ((), ())), preferred_element_type=jnp.float32
    )


def in_order(first, mine, other, axis):
    return jnp.where(
        first,
        jnp.concatenate([mine, other], axis=axis),
        jnp.concatenate([other, mine], axis=axis),
    )


def pairs_z1y0():
    return [(z1 * 8 + y, (y % 2) * 8 + (y // 2) * 2 + z1) for z1 in range(2) for y in range(8)]


def pairs_part(d1, d2):
    return [(i, i ^ (2 * d1 + d2)) for i in range(4)]


def pairs_rows():
    return [
        (z1 * 8 + z0 * 4 + c * 2 + z2, c * 8 + z1 * 4 + z2 * 2 + z0)
        for z1 in range(2)
        for z0 in range(2)
        for c in range(2)
        for z2 in range(2)
    ]


def pack(rows):
    q = rows.shape[0] // 2
    return jnp.concatenate([rows[:q], rows[q:]], axis=1)


def body(grad_parts, basis_in, basis_out, eig_in, eig_out):
    bf16, f32 = jnp.bfloat16, jnp.float32
    x, z1, z0, c, y, z2 = (lax.axis_index(a) for a in AXES)
    rows, cols = basis_in.shape
    half, quarter = rows // 2, cols // 4
    wide = 2 * rows
    low_core, low_rep, low_z1 = c == 0, z2 == 0, z1 == 0


    grad = grad_parts[0]
    parts = jnp.stack([pack(grad[:, i * quarter : (i + 1) * quarter]) for i in range(4)])

    def piece(d1, d2):
        which = 2 * (z2 ^ d2) + (z1 ^ d1)
        return lax.dynamic_index_in_dim(parts, which, 0, keepdims=False)

    def from_part(d1, d2):
        return lax.ppermute(piece(d1, d2), PART, pairs_part(d1, d2)).astype(f32)

    mine = (piece(0, 0).astype(f32) + from_part(0, 1)).astype(bf16)
    other = (from_part(1, 0) + from_part(1, 1)).astype(bf16)
    grad = in_order(low_z1, mine, other, 1)

    bi = basis_in.astype(bf16)
    bi = jnp.where(low_rep, bi[:half], bi[half:])
    bi = lax.ppermute(bi, ("z1", "z0", "c", "z2"), pairs_rows())
    bi = gather(bi, RING, 8)
    bi = in_order(low_core, bi, lax.ppermute(bi, "c", SWAP), 1).reshape(8 * rows, cols)

    bo = basis_out.astype(bf16)
    low = jnp.concatenate([bo[:, i * quarter : i * quarter + half] for i in range(4)], axis=1)
    high = jnp.concatenate([bo[:, i * quarter + half : (i + 1) * quarter] for i in range(4)], axis=1)
    low, high = pack(low), pack(high)
    bo = jnp.stack([jnp.where(low_rep, low, high), jnp.where(low_rep, high, low)])
    bo = lax.ppermute(bo, ("z1", "y"), pairs_z1y0())
    bo = lax.all_gather(bo, "y", axis=0)
    bo = bo.reshape(4, 2, 2, half, 2, wide).transpose(2, 1, 4, 3, 0, 5)
    near, far = bo.reshape(2, wide, 4 * wide)

    grad = gather(grad, "y", 8)
    grad = grad.reshape(8, half, 4, quarter).transpose(2, 1, 0, 3).reshape(wide, 8 * quarter)
    part = dot(grad, bi, 1, 0).astype(bf16).reshape(4, half, cols)
    turned = scatter_sum(part, PART).astype(bf16)
    turned = gather(turned, RING, 8)
    other = lax.ppermute(turned, "c", SWAP)
    turned = in_order(low_core, turned[:, None], other[:, None], 1).reshape(16 * half, cols)

    part = dot(near, turned, 1, 0).astype(bf16).reshape(4, half, cols)
    rotated = scatter_sum(part, PART)
    first = (((x * 2 + z1) * 2 + z0) * 2 + c) * rows + z2 * half
    out_scale = lax.dynamic_slice_in_dim(eig_out, first, half, 0)
    in_scale = lax.dynamic_slice_in_dim(eig_in, y * cols, cols, 0)
    scaled = (rotated / (out_scale[:, None] * in_scale[None, :] + DAMPING)).astype(bf16)
    scaled = gather(scaled, PART, 4).reshape(wide, cols)

    part = dot(scaled, bi, 1, 1).astype(bf16)
    part = part.reshape(4, half, 8, quarter).transpose(2, 1, 0, 3).reshape(8, half, cols)
    back = scatter_sum(part, "y").astype(bf16)
    other = lax.ppermute(back, "z1", SWAP)
    first, second = jnp.where(low_z1, back, other), jnp.where(low_z1, other, back)
    back = jnp.concatenate(
        [
            jnp.concatenate(
                [first[:, i * quarter : (i + 1) * quarter], second[:, i * quarter : (i + 1) * quarter]],
                axis=1,
            )
            for i in range(4)
        ],
        axis=0,
    )

    part = jnp.concatenate([dot(near, back, 0, 0), dot(far, back, 0, 0)], axis=1)
    part = part.reshape(8, 2, half, cols)
    keep = jnp.where(low_core, part[:, 0], part[:, 1])
    give = jnp.where(low_core, part[:, 1], part[:, 0]).astype(bf16)
    part = (keep + lax.ppermute(give, "c", SWAP).astype(f32)).astype(bf16)
    out = scatter_sum(part, RING).astype(bf16)
    return in_order(low_rep, out[:, :wide], out[:, wide:], 0)


def solution(mesh):
    fine = Mesh(mesh.devices.reshape(4, 2, 2, 2, 8, 2), AXES)
    in_specs = (P("z2", ROWS, "y"), P(ROWS, "y"), P(ROWS, "y"), P(), P())
    out_specs = P(ROWS, ("y", "z2"))
    return jax.shard_map(body, mesh=fine, in_specs=in_specs, out_specs=out_specs, check_vma=False)
```

```python
import jax
import jax.numpy as jnp
from jax import lax
from jax.sharding import Mesh, PartitionSpec as P

DAMPING = 0.1
AXES = ("x", "z1", "z0", "c", "y", "z2")
ROWS = ("x", "z1", "z0", "c")
RING = ("x", "z0")
PART = ("z1", "z2")
SWAP = [(0, 1), (1, 0)]


def gather(block, axes, count):
    return lax.all_to_all(
        jnp.broadcast_to(block[None], (count,) + block.shape), axes, 0, 0, tiled=True
    )


def scatter_sum(blocks, axes):
    got = lax.all_to_all(blocks, axes, 0, 0, tiled=True)
    return jnp.sum(got.astype(jnp.float32), axis=0)


def dot(left, right, left_dim, right_dim):
    return lax.dot_general(
        left, right, (((left_dim,), (right_dim,)), ((), ())), preferred_element_type=jnp.float32
    )


def in_order(first, mine, other, axis):
    return jnp.where(
        first,
        jnp.concatenate([mine, other], axis=axis),
        jnp.concatenate([other, mine], axis=axis),
    )


def pairs_z1y0():
    return [(z1 * 8 + y, (y % 2) * 8 + (y // 2) * 2 + z1) for z1 in range(2) for y in range(8)]


def pairs_part(d1, d2):
    return [(i, i ^ (2 * d1 + d2)) for i in range(4)]


def pairs_rows():
    return [
        (z1 * 8 + z0 * 4 + c * 2 + z2, c * 8 + z1 * 4 + z2 * 2 + z0)
        for z1 in range(2)
        for z0 in range(2)
        for c in range(2)
        for z2 in range(2)
    ]


def pack(rows):
    q = rows.shape[0] // 2
    return jnp.concatenate([rows[:q], rows[q:]], axis=1)


def body(grad_parts, basis_in, basis_out, eig_in, eig_out):
    bf16, f32 = jnp.bfloat16, jnp.float32
    x, z1, z0, c, y, z2 = (lax.axis_index(a) for a in AXES)
    rows, cols = basis_in.shape
    half, quarter = rows // 2, cols // 4
    wide = 2 * rows
    low_core, low_rep, low_z1 = c == 0, z2 == 0, z1 == 0


    bo = basis_out.astype(bf16)
    low = jnp.concatenate([bo[:, i * quarter : i * quarter + half] for i in range(4)], axis=1)
    high = jnp.concatenate([bo[:, i * quarter + half : (i + 1) * quarter] for i in range(4)], axis=1)
    low, high = pack(low), pack(high)
    bo = jnp.stack([jnp.where(low_rep, low, high), jnp.where(low_rep, high, low)])
    bo = lax.ppermute(bo, ("z1", "y"), pairs_z1y0())

    grad = grad_parts[0]
    parts = jnp.stack([pack(grad[:, i * quarter : (i + 1) * quarter]) for i in range(4)])

    def piece(d1, d2):
        which = 2 * (z2 ^ d2) + (z1 ^ d1)
        return lax.dynamic_index_in_dim(parts, which, 0, keepdims=False)

    def from_part(d1, d2):
        return lax.ppermute(piece(d1, d2), PART, pairs_part(d1, d2)).astype(f32)

    mine = (piece(0, 0).astype(f32) + from_part(0, 1)).astype(bf16)
    other = (from_part(1, 0) + from_part(1, 1)).astype(bf16)
    grad = in_order(low_z1, mine, other, 1)

    bo, grad = lax.optimization_barrier((bo, grad))
    bo = lax.all_gather(bo, "y", axis=0)
    bo = bo.reshape(4, 2, 2, half, 2, wide).transpose(2, 1, 4, 3, 0, 5)
    near, far = bo.reshape(2, wide, 4 * wide)

    bi = basis_in.astype(bf16)
    bi = jnp.where(low_rep, bi[:half], bi[half:])
    bi = lax.ppermute(bi, ("z1", "z0", "c", "z2"), pairs_rows())
    other = lax.ppermute(bi, "z0", SWAP)
    pair = in_order(z0 == 0, bi[None], other[None], 0)
    turn = [pair] + [lax.ppermute(pair, "x", [(i, (i - s) % 4) for i in range(4)]) for s in (1, 2, 3)]
    turn = jnp.concatenate(turn + turn[:3], axis=0)
    bi = lax.dynamic_slice_in_dim(turn, 2 * ((4 - x) % 4), 8, 0)
    bi = in_order(low_core, bi, lax.ppermute(bi, "c", SWAP), 1).reshape(8 * rows, cols)

    grad = gather(grad, "y", 8)
    grad = grad.reshape(8, half, 4, quarter).transpose(2, 1, 0, 3).reshape(wide, 8 * quarter)
    part = dot(grad, bi, 1, 0).astype(bf16).reshape(4, half, cols)
    turned = scatter_sum(part, PART).astype(bf16)
    turned = gather(turned, RING, 8)
    other = lax.ppermute(turned, "c", SWAP)
    turned = in_order(low_core, turned[:, None], other[:, None], 1).reshape(16 * half, cols)

    part = dot(near, turned, 1, 0).astype(bf16).reshape(4, half, cols)
    rotated = scatter_sum(part, PART)
    first = (((x * 2 + z1) * 2 + z0) * 2 + c) * rows + z2 * half
    out_scale = lax.dynamic_slice_in_dim(eig_out, first, half, 0)
    in_scale = lax.dynamic_slice_in_dim(eig_in, y * cols, cols, 0)
    scaled = (rotated / (out_scale[:, None] * in_scale[None, :] + DAMPING)).astype(bf16)
    scaled = gather(scaled, PART, 4).reshape(wide, cols)

    part = dot(scaled, bi, 1, 1).astype(bf16)
    part = part.reshape(4, half, 8, quarter).transpose(2, 1, 0, 3).reshape(8, half, cols)
    back = scatter_sum(part, "y").astype(bf16)
    other = lax.ppermute(back, "z1", SWAP)
    first, second = jnp.where(low_z1, back, other), jnp.where(low_z1, other, back)
    back = jnp.concatenate(
        [
            jnp.concatenate(
                [first[:, i * quarter : (i + 1) * quarter], second[:, i * quarter : (i + 1) * quarter]],
                axis=1,
            )
            for i in range(4)
        ],
        axis=0,
    )

    part = jnp.concatenate([dot(near, back, 0, 0), dot(far, back, 0, 0)], axis=1)
    part = part.reshape(8, 2, half, cols)
    keep = jnp.where(low_core, part[:, 0], part[:, 1])
    give = jnp.where(low_core, part[:, 1], part[:, 0]).astype(bf16)
    part = (keep + lax.ppermute(give, "c", SWAP).astype(f32)).astype(bf16)
    out = scatter_sum(part, RING).astype(bf16)
    return in_order(low_rep, out[:, :wide], out[:, wide:], 0)


def solution(mesh):
    fine = Mesh(mesh.devices.reshape(4, 2, 2, 2, 8, 2), AXES)
    in_specs = (P("z2", ROWS, "y"), P(ROWS, "y"), P(ROWS, "y"), P(), P())
    out_specs = P(ROWS, ("y", "z2"))
    return jax.shard_map(body, mesh=fine, in_specs=in_specs, out_specs=out_specs, check_vma=False)
```

```python
import jax
import jax.numpy as jnp
from jax import lax
from jax.sharding import Mesh, PartitionSpec as P

DAMPING = 0.1
AXES = ("x", "z1", "z0", "c", "y", "z2")
ROWS = ("x", "z1", "z0", "c")
RING = ("x", "z0")
PART = ("z1", "z2")
SWAP = [(0, 1), (1, 0)]


def gather(block, axes, count):
    return lax.all_to_all(
        jnp.broadcast_to(block[None], (count,) + block.shape), axes, 0, 0, tiled=True
    )


def scatter_sum(blocks, axes):
    got = lax.all_to_all(blocks, axes, 0, 0, tiled=True)
    return jnp.sum(got.astype(jnp.float32), axis=0)


def dot(left, right, left_dim, right_dim):
    return lax.dot_general(
        left, right, (((left_dim,), (right_dim,)), ((), ())), preferred_element_type=jnp.float32
    )


def in_order(first, mine, other, axis):
    return jnp.where(
        first,
        jnp.concatenate([mine, other], axis=axis),
        jnp.concatenate([other, mine], axis=axis),
    )


def pairs_z1y0():
    return [(z1 * 8 + y, (y % 2) * 8 + (y // 2) * 2 + z1) for z1 in range(2) for y in range(8)]


def pairs_part(d1, d2):
    return [(i, i ^ (2 * d1 + d2)) for i in range(4)]


def pairs_rows():
    return [
        (z1 * 8 + z0 * 4 + c * 2 + z2, c * 8 + z1 * 4 + z2 * 2 + z0)
        for z1 in range(2)
        for z0 in range(2)
        for c in range(2)
        for z2 in range(2)
    ]


def pack(rows):
    q = rows.shape[0] // 2
    return jnp.concatenate([rows[:q], rows[q:]], axis=1)


def body(grad_parts, basis_in, basis_out, eig_in, eig_out):
    bf16, f32 = jnp.bfloat16, jnp.float32
    x, z1, z0, c, y, z2 = (lax.axis_index(a) for a in AXES)
    rows, cols = basis_in.shape
    half, quarter = rows // 2, cols // 4
    wide = 2 * rows
    low_core, low_rep, low_z1 = c == 0, z2 == 0, z1 == 0


    bo = basis_out.astype(bf16)
    low = jnp.concatenate([bo[:, i * quarter : i * quarter + half] for i in range(4)], axis=1)
    high = jnp.concatenate([bo[:, i * quarter + half : (i + 1) * quarter] for i in range(4)], axis=1)
    low, high = pack(low), pack(high)
    bo = jnp.stack([jnp.where(low_rep, low, high), jnp.where(low_rep, high, low)])
    bo = lax.ppermute(bo, ("z1", "y"), pairs_z1y0())

    grad = grad_parts[0]
    parts = jnp.stack([pack(grad[:, i * quarter : (i + 1) * quarter]) for i in range(4)])

    def piece(d1, d2):
        which = 2 * (z2 ^ d2) + (z1 ^ d1)
        return lax.dynamic_index_in_dim(parts, which, 0, keepdims=False)

    def from_part(d1, d2):
        return lax.ppermute(piece(d1, d2), PART, pairs_part(d1, d2)).astype(f32)

    mine = (piece(0, 0).astype(f32) + from_part(0, 1)).astype(bf16)
    other = (from_part(1, 0) + from_part(1, 1)).astype(bf16)
    grad = in_order(low_z1, mine, other, 1)

    bi = basis_in.astype(bf16)
    bi = jnp.where(low_rep, bi[:half], bi[half:])
    bi = lax.ppermute(bi, ("z1", "z0", "c", "z2"), pairs_rows())

    bo, bi, grad = lax.optimization_barrier((bo, bi, grad))
    bi = gather(bi, RING, 8)
    bi = in_order(low_core, bi, lax.ppermute(bi, "c", SWAP), 1).reshape(8 * rows, cols)
    bo = lax.all_gather(bo, "y", axis=0)

    grad = gather(grad, "y", 8)
    grad = grad.reshape(8, half, 4, quarter).transpose(2, 1, 0, 3).reshape(wide, 8 * quarter)
    part = dot(grad, bi, 1, 0).astype(bf16).reshape(4, half, cols)
    turned = scatter_sum(part, PART).astype(bf16)

    bo, turned = lax.optimization_barrier((bo, turned))
    bo = bo.reshape(4, 2, 2, half, 2, wide).transpose(2, 1, 4, 3, 0, 5)
    near, far = bo.reshape(2, wide, 4 * wide)
    turned = gather(turned, RING, 8)
    other = lax.ppermute(turned, "c", SWAP)
    turned = in_order(low_core, turned[:, None], other[:, None], 1).reshape(16 * half, cols)

    part = dot(near, turned, 1, 0).astype(bf16).reshape(4, half, cols)
    rotated = scatter_sum(part, PART)
    first = (((x * 2 + z1) * 2 + z0) * 2 + c) * rows + z2 * half
    out_scale = lax.dynamic_slice_in_dim(eig_out, first, half, 0)
    in_scale = lax.dynamic_slice_in_dim(eig_in, y * cols, cols, 0)
    scaled = (rotated / (out_scale[:, None] * in_scale[None, :] + DAMPING)).astype(bf16)
    scaled = gather(scaled, PART, 4).reshape(wide, cols)

    part = dot(scaled, bi, 1, 1).astype(bf16)
    part = part.reshape(4, half, 8, quarter).transpose(2, 1, 0, 3).reshape(8, half, cols)
    back = scatter_sum(part, "y").astype(bf16)
    other = lax.ppermute(back, "z1", SWAP)
    first, second = jnp.where(low_z1, back, other), jnp.where(low_z1, other, back)
    back = jnp.concatenate(
        [
            jnp.concatenate(
                [first[:, i * quarter : (i + 1) * quarter], second[:, i * quarter : (i + 1) * quarter]],
                axis=1,
            )
            for i in range(4)
        ],
        axis=0,
    )

    part = jnp.concatenate(
        [dot(near, back, 0, 0).astype(bf16), dot(far, back, 0, 0).astype(bf16)], axis=1
    )
    part = part.reshape(8, 2, half, cols)
    keep = jnp.where(low_core, part[:, 0], part[:, 1])
    give = jnp.where(low_core, part[:, 1], part[:, 0])
    part = (keep.astype(f32) + lax.ppermute(give, "c", SWAP).astype(f32)).astype(bf16)
    out = scatter_sum(part, RING).astype(bf16)
    return in_order(low_rep, out[:, :wide], out[:, wide:], 0)


def solution(mesh):
    fine = Mesh(mesh.devices.reshape(4, 2, 2, 2, 8, 2), AXES)
    in_specs = (P("z2", ROWS, "y"), P(ROWS, "y"), P(ROWS, "y"), P(), P())
    out_specs = P(ROWS, ("y", "z2"))
    return jax.shard_map(body, mesh=fine, in_specs=in_specs, out_specs=out_specs, check_vma=False)
```

```python
import jax
import jax.numpy as jnp
from jax import lax
from jax.experimental import pallas as pl
from jax.experimental.pallas import tpu as pltpu
from jax.sharding import Mesh, PartitionSpec as P

DAMPING = 0.1
AXES = ("x", "z1", "z0", "c", "y", "z2")
ROWS = ("x", "z1", "z0", "c")
RING = ("x", "z0")
PART = ("z1", "z2")
SWAP = [(0, 1), (1, 0)]


def gather(block, axes, count):
    return lax.all_to_all(
        jnp.broadcast_to(block[None], (count,) + block.shape), axes, 0, 0, tiled=True
    )


def scatter_sum(blocks, axes):
    got = lax.all_to_all(blocks, axes, 0, 0, tiled=True)
    return jnp.sum(got.astype(jnp.float32), axis=0)


def dot(left, right, left_dim, right_dim):
    return lax.dot_general(
        left, right, (((left_dim,), (right_dim,)), ((), ())), preferred_element_type=jnp.float32
    )


def in_order(first, mine, other, axis):
    return jnp.where(
        first,
        jnp.concatenate([mine, other], axis=axis),
        jnp.concatenate([other, mine], axis=axis),
    )


def pairs_z1y0():
    return [(z1 * 8 + y, (y % 2) * 8 + (y // 2) * 2 + z1) for z1 in range(2) for y in range(8)]


def pairs_part(d1, d2):
    return [(i, i ^ (2 * d1 + d2)) for i in range(4)]


def pairs_rows():
    return [
        (z1 * 8 + z0 * 4 + c * 2 + z2, c * 8 + z1 * 4 + z2 * 2 + z0)
        for z1 in range(2)
        for z0 in range(2)
        for c in range(2)
        for z2 in range(2)
    ]


def pack(rows):
    q = rows.shape[0] // 2
    return jnp.concatenate([rows[:q], rows[q:]], axis=1)


def run(kernel, outs, args, scratch=(), flags=0):
    size = sum(a.size * a.dtype.itemsize for a in (*args, *jax.tree.leaves(outs)))
    return pl.pallas_call(
        kernel,
        out_shape=outs,
        in_specs=[
            pl.BlockSpec(memory_space=pltpu.SMEM if i < flags else pltpu.VMEM)
            for i in range(len(args))
        ],
        scratch_shapes=[pltpu.VMEM(shape, jnp.bfloat16) for shape in scratch],
        cost_estimate=pl.CostEstimate(flops=2 * 288 * 1152 * 576, bytes_accessed=size, transcendentals=0),
        compiler_params=pltpu.CompilerParams(vmem_limit_bytes=32 * 2**20),
    )(*args)


def shape(*dims):
    return jax.ShapeDtypeStruct(dims, jnp.bfloat16)


def order_out(core, rep, rows, out):
    q = out.shape[1]
    low_core, low_rep = core[0] == 0, rep[0] == 0
    for a in range(2):
        block = rows[q * a : q * a + q].astype(jnp.bfloat16).astype(jnp.float32)
        for t in range(4):
            def cut(block_c, half):
                at = (4 * (t // 2) + 2 * block_c + half) * q
                return block[:, at : at + q]

            for far in range(2):
                first = jnp.where(low_core, cut(t % 2, far), cut(1 - t % 2, far))
                second = jnp.where(low_core, cut(t % 2, 1 - far), cut(1 - t % 2, 1 - far))
                at = (4 * a + t) * q
                out[far, :, at : at + q] = jnp.where(low_rep, first, second).astype(jnp.bfloat16)


def turn_in(grad, basis, out, left):
    count, _, wide = grad.shape
    q = wide // 4
    for y in range(count):
        for g in range(4):
            left[g, :, q * y : q * y + q] = grad[y, :, q * g : q * g + q]
    right = basis[...].reshape(count * q, basis.shape[2])
    for g in range(4):
        out[g] = dot(left[g], right, 1, 0).astype(out.dtype)


def turn_out(rows, own, other, out, left, right):
    q, wide = own.shape[1], rows.shape[3] // 2
    for x in range(4):
        for b in range(2):
            for h in range(2):
                left[2 * b + h, :, wide * x : wide * x + wide] = rows[
                    2 * x + b, 0, :, wide * h : wide * h + wide
                ]
    for i in range(8):
        right[2 * q * i : 2 * q * i + q] = own[i]
        right[2 * q * i + q : 2 * q * i + 2 * q] = other[i]
    right = right[...]
    for g in range(4):
        out[g] = dot(left[g], right, 1, 0).astype(out.dtype)


def back_in(scaled, basis, out):
    q = basis.shape[1]
    for y in range(basis.shape[0]):
        for g in range(4):
            out[y, :, q * g : q * g + q] = dot(scaled[g], basis[y], 1, 1).astype(out.dtype)


def back_out(part, rows, mine, other, keep, give, right):
    q, wide = mine.shape[0], mine.shape[1] // 2
    low = part[0] == 0
    for g in range(4):
        a = mine[:, wide // 2 * g : wide // 2 * (g + 1)]
        b = other[:, wide // 2 * g : wide // 2 * (g + 1)]
        right[g, :, : wide // 2] = jnp.where(low, a, b)
        right[g, :, wide // 2 :] = jnp.where(low, b, a)
    for x in range(4):
        for n in range(2):
            total = jnp.zeros((wide, wide), jnp.float32)
            for b in range(2):
                for h in range(2):
                    left = rows[2 * x + b, n, :, wide * h : wide * h + wide]
                    total += dot(left, right[2 * b + h], 0, 0)
            total = total.astype(keep.dtype)
            for z in range(2):
                at = 2 * q * z
                keep[2 * x + z, :, wide * n : wide * n + wide] = total[at : at + q]
                give[2 * x + z, :, wide * n : wide * n + wide] = total[at + q : at + 2 * q]


def body(grad_parts, basis_in, basis_out, eig_in, eig_out):
    bf16, f32 = jnp.bfloat16, jnp.float32
    x, z1, z0, c, y, z2 = (lax.axis_index(a) for a in AXES)
    rows, cols = basis_in.shape
    half, quarter = rows // 2, cols // 4
    wide = 2 * rows
    low_core, low_rep, low_z1 = c == 0, z2 == 0, z1 == 0


    core, rep, part_z1 = (i.astype(jnp.int32).reshape(1) for i in (c, z2, z1))

    bo = run(order_out, shape(2, half, cols), (core, rep, basis_out), flags=2)
    bo = lax.ppermute(bo, ("z1", "y"), pairs_z1y0())

    grad = grad_parts[0]
    parts = jnp.stack([pack(grad[:, i * quarter : (i + 1) * quarter]) for i in range(4)])

    def piece(d1, d2):
        which = 2 * (z2 ^ d2) + (z1 ^ d1)
        return lax.dynamic_index_in_dim(parts, which, 0, keepdims=False)

    def from_part(d1, d2):
        return lax.ppermute(piece(d1, d2), PART, pairs_part(d1, d2)).astype(f32)

    mine = (piece(0, 0).astype(f32) + from_part(0, 1)).astype(bf16)
    other = (from_part(1, 0) + from_part(1, 1)).astype(bf16)
    grad = in_order(low_z1, mine, other, 1)

    bi = basis_in.astype(bf16)
    bi = jnp.where(low_rep, bi[:half], bi[half:])
    bi = lax.ppermute(bi, ("z1", "z0", "c", "z2"), pairs_rows())
    bi = gather(bi, RING, 8)
    bi = in_order(low_core, bi, lax.ppermute(bi, "c", SWAP), 1)

    bo, grad = lax.optimization_barrier((bo, grad))
    grad = gather(grad, "y", 8)
    bo, grad = lax.optimization_barrier((bo, grad))
    bo = lax.all_gather(bo, "y", axis=0)

    left = (4, half, 8 * quarter)
    part = run(turn_in, shape(4, half, cols), (grad, bi), (left,))
    turned = scatter_sum(part, PART).astype(bf16)
    turned = gather(turned, RING, 8)
    other = lax.ppermute(turned, "c", SWAP)

    right = (8 * rows, cols)
    part = run(turn_out, shape(4, half, cols), (bo, turned, other), (left, right))
    rotated = scatter_sum(part, PART)
    first = (((x * 2 + z1) * 2 + z0) * 2 + c) * rows + z2 * half
    out_scale = lax.dynamic_slice_in_dim(eig_out, first, half, 0)
    in_scale = lax.dynamic_slice_in_dim(eig_in, y * cols, cols, 0)
    scaled = (rotated / (out_scale[:, None] * in_scale[None, :] + DAMPING)).astype(bf16)
    scaled = gather(scaled, PART, 4)

    part = run(back_in, shape(8, half, cols), (scaled, bi))
    back = scatter_sum(part, "y").astype(bf16)
    other = lax.ppermute(back, "z1", SWAP)

    keep, give = run(
        back_out,
        (shape(8, half, cols), shape(8, half, cols)),
        (part_z1, bo, back, other),
        ((4, half, wide),),
        flags=1,
    )
    part = (keep.astype(f32) + lax.ppermute(give, "c", SWAP).astype(f32)).astype(bf16)
    out = scatter_sum(part, RING).astype(bf16)
    return in_order(low_rep, out[:, :wide], out[:, wide:], 0)


def solution(mesh):
    fine = Mesh(mesh.devices.reshape(4, 2, 2, 2, 8, 2), AXES)
    in_specs = (P("z2", ROWS, "y"), P(ROWS, "y"), P(ROWS, "y"), P(), P())
    out_specs = P(ROWS, ("y", "z2"))
    return jax.shard_map(body, mesh=fine, in_specs=in_specs, out_specs=out_specs, check_vma=False)
```

```python
import jax
import jax.numpy as jnp
from jax import lax
from jax.experimental import pallas as pl
from jax.experimental.pallas import tpu as pltpu
from jax.sharding import Mesh, PartitionSpec as P

DAMPING = 0.1
AXES = ("x", "z1", "z0", "c", "y", "z2")
ROWS = ("x", "z1", "z0", "c")
RING = ("x", "z0")
PART = ("z1", "z2")
SWAP = [(0, 1), (1, 0)]


def gather(block, axes, count):
    return lax.all_to_all(
        jnp.broadcast_to(block[None], (count,) + block.shape), axes, 0, 0, tiled=True
    )


def scatter_sum(blocks, axes):
    got = lax.all_to_all(blocks, axes, 0, 0, tiled=True)
    return jnp.sum(got.astype(jnp.float32), axis=0)


def dot(left, right, left_dim, right_dim):
    return lax.dot_general(
        left, right, (((left_dim,), (right_dim,)), ((), ())), preferred_element_type=jnp.float32
    )


def in_order(first, mine, other, axis):
    return jnp.where(
        first,
        jnp.concatenate([mine, other], axis=axis),
        jnp.concatenate([other, mine], axis=axis),
    )


def pairs_part(d1, d2):
    return [(i, i ^ (2 * d1 + d2)) for i in range(4)]


def pairs_rows():
    return [
        (z1 * 8 + z0 * 4 + c * 2 + z2, c * 8 + z1 * 4 + z2 * 2 + z0)
        for z1 in range(2)
        for z0 in range(2)
        for c in range(2)
        for z2 in range(2)
    ]


def pack(rows):
    q = rows.shape[0] // 2
    return jnp.concatenate([rows[:q], rows[q:]], axis=1)


def run(kernel, outs, args, scratch=(), flags=0):
    size = sum(a.size * a.dtype.itemsize for a in (*args, *jax.tree.leaves(outs)))
    return pl.pallas_call(
        kernel,
        out_shape=outs,
        in_specs=[
            pl.BlockSpec(memory_space=pltpu.SMEM if i < flags else pltpu.VMEM)
            for i in range(len(args))
        ],
        scratch_shapes=[pltpu.VMEM(shape, jnp.bfloat16) for shape in scratch],
        cost_estimate=pl.CostEstimate(flops=2 * 288 * 1152 * 576, bytes_accessed=size, transcendentals=0),
        compiler_params=pltpu.CompilerParams(vmem_limit_bytes=32 * 2**20),
    )(*args)


def shape(*dims):
    return jax.ShapeDtypeStruct(dims, jnp.bfloat16)


def order_out(core, rep, rows, out):
    q = out.shape[1]
    low_core, low_rep = core[0] == 0, rep[0] == 0
    for a in range(2):
        block = rows[q * a : q * a + q].astype(jnp.bfloat16).astype(jnp.float32)
        for t in range(4):
            def cut(block_c, half):
                at = (4 * (t // 2) + 2 * block_c + half) * q
                return block[:, at : at + q]

            for far in range(2):
                first = jnp.where(low_core, cut(t % 2, far), cut(1 - t % 2, far))
                second = jnp.where(low_core, cut(t % 2, 1 - far), cut(1 - t % 2, 1 - far))
                at = (4 * a + t) * q
                out[far, :, at : at + q] = jnp.where(low_rep, first, second).astype(jnp.bfloat16)


def turn_in(grad, basis, out, left):
    count, _, wide = grad.shape
    q = wide // 4
    for y in range(count):
        for g in range(4):
            left[g, :, q * y : q * y + q] = grad[y, :, q * g : q * g + q]
    right = basis[...].reshape(count * q, basis.shape[2])
    for g in range(4):
        out[g] = dot(left[g], right, 1, 0).astype(out.dtype)


def turn_out(part, rows, near, own, other, out, left, right):
    q, wide = own.shape[1], rows.shape[3] // 2
    z1 = part[0]
    for x in range(4):
        for h in range(2):
            at, cut = wide * x, wide * h
            left[h, :, at : at + wide] = rows[2 * x + z1, 0, :, cut : cut + wide]
            left[2 + h, :, at : at + wide] = near[x, :, cut : cut + wide]
    for i in range(8):
        right[2 * q * i : 2 * q * i + q] = own[i]
        right[2 * q * i + q : 2 * q * i + 2 * q] = other[i]
    right = right[...]
    for h in range(2):
        out[2 * z1 + h] = dot(left[h], right, 1, 0).astype(out.dtype)
        out[2 * (1 - z1) + h] = dot(left[2 + h], right, 1, 0).astype(out.dtype)


def back_in(scaled, basis, out):
    q = basis.shape[1]
    for y in range(basis.shape[0]):
        for g in range(4):
            out[y, :, q * g : q * g + q] = dot(scaled[g], basis[y], 1, 1).astype(out.dtype)


def back_out(part, rows, near, far, mine, other, keep, give, right):
    q, wide = mine.shape[0], mine.shape[1] // 2
    z1 = part[0]
    low = z1 == 0
    for g in range(4):
        a = mine[:, wide // 2 * g : wide // 2 * (g + 1)]
        b = other[:, wide // 2 * g : wide // 2 * (g + 1)]
        right[g, :, : wide // 2] = jnp.where(low, a, b)
        right[g, :, wide // 2 :] = jnp.where(low, b, a)
    for x in range(4):
        for n in range(2):
            total = jnp.zeros((wide, wide), jnp.float32)
            for h in range(2):
                cut = wide * h
                left = rows[2 * x + z1, n, :, cut : cut + wide]
                total += dot(left, right[2 * z1 + h], 0, 0)
                left = (near, far)[n][x, :, cut : cut + wide]
                total += dot(left, right[2 * (1 - z1) + h], 0, 0)
            total = total.astype(keep.dtype)
            for z in range(2):
                at = 2 * q * z
                keep[2 * x + z, :, wide * n : wide * n + wide] = total[at : at + q]
                give[2 * x + z, :, wide * n : wide * n + wide] = total[at + q : at + 2 * q]


def body(grad_parts, basis_in, basis_out, eig_in, eig_out):
    bf16, f32 = jnp.bfloat16, jnp.float32
    x, z1, z0, c, y, z2 = (lax.axis_index(a) for a in AXES)
    rows, cols = basis_in.shape
    half, quarter = rows // 2, cols // 4
    wide = 2 * rows
    low_core, low_rep, low_z1 = c == 0, z2 == 0, z1 == 0


    core, rep, part_z1 = (i.astype(jnp.int32).reshape(1) for i in (c, z2, z1))

    bo = run(order_out, shape(2, half, cols), (core, rep, basis_out), flags=2)
    bo, grad_parts = lax.optimization_barrier((bo, grad_parts))
    bo = lax.all_gather(bo, "y", axis=0)

    grad = grad_parts[0]
    parts = jnp.stack([pack(grad[:, i * quarter : (i + 1) * quarter]) for i in range(4)])

    def piece(d1, d2):
        which = 2 * (z2 ^ d2) + (z1 ^ d1)
        return lax.dynamic_index_in_dim(parts, which, 0, keepdims=False)

    def from_part(d1, d2):
        return lax.ppermute(piece(d1, d2), PART, pairs_part(d1, d2)).astype(f32)

    mine = (piece(0, 0).astype(f32) + from_part(0, 1)).astype(bf16)
    other = (from_part(1, 0) + from_part(1, 1)).astype(bf16)
    grad = in_order(low_z1, mine, other, 1)

    bi = basis_in.astype(bf16)
    bi = jnp.where(low_rep, bi[:half], bi[half:])
    bi = lax.ppermute(bi, ("z1", "z0", "c", "z2"), pairs_rows())
    bi = gather(bi, RING, 8)
    bi = in_order(low_core, bi, lax.ppermute(bi, "c", SWAP), 1)

    bo, grad = lax.optimization_barrier((bo, grad))
    by_z1 = bo.reshape(4, 2, 2, half, cols)

    def from_other_z1(far):
        block = lax.dynamic_index_in_dim(by_z1[:, :, far], 1 - z1, 1, keepdims=False)
        return lax.ppermute(block, "z1", SWAP)

    near, far = from_other_z1(0), from_other_z1(1)

    grad = gather(grad, "y", 8)
    left = (4, half, 8 * quarter)
    part = run(turn_in, shape(4, half, cols), (grad, bi), (left,))
    near, part = lax.optimization_barrier((near, part))
    turned = scatter_sum(part, PART).astype(bf16)
    turned = gather(turned, RING, 8)
    other = lax.ppermute(turned, "c", SWAP)

    right = (8 * rows, cols)
    part = run(turn_out, shape(4, half, cols), (part_z1, bo, near, turned, other), (left, right), 1)
    rotated = scatter_sum(part, PART)
    first = (((x * 2 + z1) * 2 + z0) * 2 + c) * rows + z2 * half
    out_scale = lax.dynamic_slice_in_dim(eig_out, first, half, 0)
    in_scale = lax.dynamic_slice_in_dim(eig_in, y * cols, cols, 0)
    scaled = (rotated / (out_scale[:, None] * in_scale[None, :] + DAMPING)).astype(bf16)
    scaled = gather(scaled, PART, 4)

    part = run(back_in, shape(8, half, cols), (scaled, bi))
    back = scatter_sum(part, "y").astype(bf16)
    far, back = lax.optimization_barrier((far, back))
    other = lax.ppermute(back, "z1", SWAP)

    keep, give = run(
        back_out,
        (shape(8, half, cols), shape(8, half, cols)),
        (part_z1, bo, near, far, back, other),
        ((4, half, wide),),
        flags=1,
    )
    part = (keep.astype(f32) + lax.ppermute(give, "c", SWAP).astype(f32)).astype(bf16)
    out = scatter_sum(part, RING).astype(bf16)
    return in_order(low_rep, out[:, :wide], out[:, wide:], 0)


def solution(mesh):
    fine = Mesh(mesh.devices.reshape(4, 2, 2, 2, 8, 2), AXES)
    in_specs = (P("z2", ROWS, "y"), P(ROWS, "y"), P(ROWS, "y"), P(), P())
    out_specs = P(ROWS, ("y", "z2"))
    return jax.shard_map(body, mesh=fine, in_specs=in_specs, out_specs=out_specs, check_vma=False)
```

```python
import jax
import jax.numpy as jnp
from jax import lax
from jax.experimental import pallas as pl
from jax.experimental.pallas import tpu as pltpu
from jax.sharding import Mesh, PartitionSpec as P

DAMPING = 0.1
AXES = ("x", "z1", "z0", "c", "y", "z2")
ROWS = ("x", "z1", "z0", "c")
RING = ("x", "z0")
PART = ("z1", "z2")
SWAP = [(0, 1), (1, 0)]


def gather(block, axes, count):
    return lax.all_to_all(
        jnp.broadcast_to(block[None], (count,) + block.shape), axes, 0, 0, tiled=True
    )


def scatter_sum(blocks, axes):
    got = lax.all_to_all(blocks, axes, 0, 0, tiled=True)
    return jnp.sum(got.astype(jnp.float32), axis=0)


def dot(left, right, left_dim, right_dim):
    return lax.dot_general(
        left, right, (((left_dim,), (right_dim,)), ((), ())), preferred_element_type=jnp.float32
    )


def in_order(first, mine, other, axis):
    return jnp.where(
        first,
        jnp.concatenate([mine, other], axis=axis),
        jnp.concatenate([other, mine], axis=axis),
    )


def pairs_z1y0():
    return [(z1 * 8 + y, (y % 2) * 8 + (y // 2) * 2 + z1) for z1 in range(2) for y in range(8)]


def pairs_part(d1, d2):
    return [(i, i ^ (2 * d1 + d2)) for i in range(4)]


def pairs_rows():
    return [
        (z1 * 8 + z0 * 4 + c * 2 + z2, c * 8 + z1 * 4 + z2 * 2 + z0)
        for z1 in range(2)
        for z0 in range(2)
        for c in range(2)
        for z2 in range(2)
    ]


def pack(rows):
    q = rows.shape[0] // 2
    return jnp.concatenate([rows[:q], rows[q:]], axis=1)


def run(kernel, outs, args, scratch=(), flags=0):
    size = sum(a.size * a.dtype.itemsize for a in (*args, *jax.tree.leaves(outs)))
    return pl.pallas_call(
        kernel,
        out_shape=outs,
        in_specs=[
            pl.BlockSpec(memory_space=pltpu.SMEM if i < flags else pltpu.VMEM)
            for i in range(len(args))
        ],
        scratch_shapes=[pltpu.VMEM(shape, jnp.bfloat16) for shape in scratch],
        cost_estimate=pl.CostEstimate(flops=2 * 288 * 1152 * 576, bytes_accessed=size, transcendentals=0),
        compiler_params=pltpu.CompilerParams(vmem_limit_bytes=32 * 2**20),
    )(*args)


def shape(*dims):
    return jax.ShapeDtypeStruct(dims, jnp.bfloat16)


def order_out(core, rep, rows, out):
    q = out.shape[1]
    low_core, low_rep = core[0] == 0, rep[0] == 0
    for a in range(2):
        block = rows[q * a : q * a + q].astype(jnp.bfloat16).astype(jnp.float32)
        for t in range(4):
            def cut(block_c, half):
                at = (4 * (t // 2) + 2 * block_c + half) * q
                return block[:, at : at + q]

            for far in range(2):
                first = jnp.where(low_core, cut(t % 2, far), cut(1 - t % 2, far))
                second = jnp.where(low_core, cut(t % 2, 1 - far), cut(1 - t % 2, 1 - far))
                at = (4 * a + t) * q
                out[far, :, at : at + q] = jnp.where(low_rep, first, second).astype(jnp.bfloat16)


def turn_in(grad, basis, out, left):
    count, _, wide = grad.shape
    q = wide // 4
    for y in range(count):
        for g in range(4):
            left[g, :, q * y : q * y + q] = grad[y, :, q * g : q * g + q]
    right = basis[...].reshape(count * q, basis.shape[2])
    for g in range(4):
        out[g] = dot(left[g], right, 1, 0).astype(out.dtype)


def turn_out(rows, own, other, out, left, right):
    q, wide = own.shape[1], rows.shape[3] // 2
    for x in range(4):
        for b in range(2):
            for h in range(2):
                left[2 * b + h, :, wide * x : wide * x + wide] = rows[
                    2 * x + b, 0, :, wide * h : wide * h + wide
                ]
    for i in range(8):
        right[2 * q * i : 2 * q * i + q] = own[i]
        right[2 * q * i + q : 2 * q * i + 2 * q] = other[i]
    right = right[...]
    for g in range(4):
        out[g] = dot(left[g], right, 1, 0).astype(out.dtype)


def back_in(scaled, basis, out):
    q = basis.shape[1]
    for y in range(basis.shape[0]):
        for g in range(4):
            out[y, :, q * g : q * g + q] = dot(scaled[g], basis[y], 1, 1).astype(out.dtype)


def back_out(part, rows, mine, other, keep, give, right):
    q, wide = mine.shape[0], mine.shape[1] // 2
    low = part[0] == 0
    for g in range(4):
        a = mine[:, wide // 2 * g : wide // 2 * (g + 1)]
        b = other[:, wide // 2 * g : wide // 2 * (g + 1)]
        right[g, :, : wide // 2] = jnp.where(low, a, b)
        right[g, :, wide // 2 :] = jnp.where(low, b, a)
    for x in range(4):
        for n in range(2):
            total = jnp.zeros((wide, wide), jnp.float32)
            for b in range(2):
                for h in range(2):
                    left = rows[2 * x + b, n, :, wide * h : wide * h + wide]
                    total += dot(left, right[2 * b + h], 0, 0)
            total = total.astype(keep.dtype)
            for z in range(2):
                at = 2 * q * z
                keep[2 * x + z, :, wide * n : wide * n + wide] = total[at : at + q]
                give[2 * x + z, :, wide * n : wide * n + wide] = total[at + q : at + 2 * q]


def body(grad_parts, basis_in, basis_out, eig_in, eig_out):
    bf16, f32 = jnp.bfloat16, jnp.float32
    x, z1, z0, c, y, z2 = (lax.axis_index(a) for a in AXES)
    rows, cols = basis_in.shape
    half, quarter = rows // 2, cols // 4
    wide = 2 * rows
    low_core, low_rep, low_z1 = c == 0, z2 == 0, z1 == 0


    core, rep, part_z1 = (i.astype(jnp.int32).reshape(1) for i in (c, z2, z1))

    bo = run(order_out, shape(2, half, cols), (core, rep, basis_out), flags=2)
    bo, grad_parts, basis_in = lax.optimization_barrier((bo, grad_parts, basis_in))
    bo = lax.ppermute(bo, ("z1", "y"), pairs_z1y0())

    bi = basis_in.astype(bf16)
    bi = jnp.where(low_rep, bi[:half], bi[half:])
    bi = lax.ppermute(bi, ("z1", "z0", "c", "z2"), pairs_rows())
    bo, bi = lax.optimization_barrier((bo, bi))
    bo = lax.all_gather(bo, "y", axis=0)

    grad = grad_parts[0]
    parts = jnp.stack([pack(grad[:, i * quarter : (i + 1) * quarter]) for i in range(4)])

    def piece(d1, d2):
        which = 2 * (z2 ^ d2) + (z1 ^ d1)
        return lax.dynamic_index_in_dim(parts, which, 0, keepdims=False)

    def from_part(d1, d2):
        return lax.ppermute(piece(d1, d2), PART, pairs_part(d1, d2)).astype(f32)

    mine = (piece(0, 0).astype(f32) + from_part(0, 1)).astype(bf16)
    other = (from_part(1, 0) + from_part(1, 1)).astype(bf16)
    grad = in_order(low_z1, mine, other, 1)

    bi = gather(bi, RING, 8)
    bi = in_order(low_core, bi, lax.ppermute(bi, "c", SWAP), 1)

    grad = gather(grad, "y", 8)

    left = (4, half, 8 * quarter)
    part = run(turn_in, shape(4, half, cols), (grad, bi), (left,))
    turned = scatter_sum(part, PART).astype(bf16)
    bo, turned = lax.optimization_barrier((bo, turned))
    turned = gather(turned, RING, 8)
    other = lax.ppermute(turned, "c", SWAP)

    right = (8 * rows, cols)
    part = run(turn_out, shape(4, half, cols), (bo, turned, other), (left, right))
    rotated = scatter_sum(part, PART)
    first = (((x * 2 + z1) * 2 + z0) * 2 + c) * rows + z2 * half
    out_scale = lax.dynamic_slice_in_dim(eig_out, first, half, 0)
    in_scale = lax.dynamic_slice_in_dim(eig_in, y * cols, cols, 0)
    scaled = (rotated / (out_scale[:, None] * in_scale[None, :] + DAMPING)).astype(bf16)
    scaled = gather(scaled, PART, 4)

    part = run(back_in, shape(8, half, cols), (scaled, bi))
    back = scatter_sum(part, "y").astype(bf16)
    other = lax.ppermute(back, "z1", SWAP)

    keep, give = run(
        back_out,
        (shape(8, half, cols), shape(8, half, cols)),
        (part_z1, bo, back, other),
        ((4, half, wide),),
        flags=1,
    )
    part = (keep.astype(f32) + lax.ppermute(give, "c", SWAP).astype(f32)).astype(bf16)
    out = scatter_sum(part, RING).astype(bf16)
    return in_order(low_rep, out[:, :wide], out[:, wide:], 0)


def solution(mesh):
    fine = Mesh(mesh.devices.reshape(4, 2, 2, 2, 8, 2), AXES)
    in_specs = (P("z2", ROWS, "y"), P(ROWS, "y"), P(ROWS, "y"), P(), P())
    out_specs = P(ROWS, ("y", "z2"))
    return jax.shard_map(body, mesh=fine, in_specs=in_specs, out_specs=out_specs, check_vma=False)
```

```python
import jax
import jax.numpy as jnp
from jax import lax
from jax.experimental import pallas as pl
from jax.experimental.pallas import tpu as pltpu
from jax.sharding import Mesh, PartitionSpec as P

DAMPING = 0.1
AXES = ("x", "z1", "z0", "c", "y", "z2")
ROWS = ("x", "z1", "z0", "c")
RING = ("x", "z0")
PART = ("z1", "z2")
SWAP = [(0, 1), (1, 0)]


def gather(block, axes, count):
    return lax.all_to_all(
        jnp.broadcast_to(block[None], (count,) + block.shape), axes, 0, 0, tiled=True
    )


def scatter_sum(blocks, axes):
    got = lax.all_to_all(blocks, axes, 0, 0, tiled=True)
    return jnp.sum(got.astype(jnp.float32), axis=0)


def dot(left, right, left_dim, right_dim):
    return lax.dot_general(
        left, right, (((left_dim,), (right_dim,)), ((), ())), preferred_element_type=jnp.float32
    )


def in_order(first, mine, other, axis):
    return jnp.where(
        first,
        jnp.concatenate([mine, other], axis=axis),
        jnp.concatenate([other, mine], axis=axis),
    )


def pairs_z1y0():
    return [(z1 * 8 + y, (y % 2) * 8 + (y // 2) * 2 + z1) for z1 in range(2) for y in range(8)]


def pairs_rows():
    return [
        (z1 * 8 + z0 * 4 + c * 2 + z2, c * 8 + z1 * 4 + z2 * 2 + z0)
        for z1 in range(2)
        for z0 in range(2)
        for c in range(2)
        for z2 in range(2)
    ]


def run(kernel, outs, args, scratch=(), flags=0):
    size = sum(a.size * a.dtype.itemsize for a in (*args, *jax.tree.leaves(outs)))
    return pl.pallas_call(
        kernel,
        out_shape=outs,
        in_specs=[
            pl.BlockSpec(memory_space=pltpu.SMEM if i < flags else pltpu.VMEM)
            for i in range(len(args))
        ],
        scratch_shapes=[pltpu.VMEM(shape, jnp.bfloat16) for shape in scratch],
        cost_estimate=pl.CostEstimate(flops=2 * 288 * 1152 * 576, bytes_accessed=size, transcendentals=0),
        compiler_params=pltpu.CompilerParams(vmem_limit_bytes=32 * 2**20),
    )(*args)


def shape(*dims):
    return jax.ShapeDtypeStruct(dims, jnp.bfloat16)


def order_out(core, rep, rows, out):
    q = out.shape[1]
    low_core, low_rep = core[0] == 0, rep[0] == 0
    for a in range(2):
        block = rows[q * a : q * a + q].astype(jnp.bfloat16).astype(jnp.float32)
        for t in range(4):
            def cut(block_c, half):
                at = (4 * (t // 2) + 2 * block_c + half) * q
                return block[:, at : at + q]

            for far in range(2):
                first = jnp.where(low_core, cut(t % 2, far), cut(1 - t % 2, far))
                second = jnp.where(low_core, cut(t % 2, 1 - far), cut(1 - t % 2, 1 - far))
                at = (4 * a + t) * q
                out[far, :, at : at + q] = jnp.where(low_rep, first, second).astype(jnp.bfloat16)


def cut_grad(grad, out):
    q, wide = grad.shape[0] // 2, grad.shape[1] // 4
    for part, block in enumerate((0, 2, 1, 3)):
        for h in range(2):
            piece = grad[q * h : q * h + q, wide * block : wide * block + wide]
            out[part, :, wide * h : wide * h + wide] = piece


def join_grad(got, out):
    wide = got.shape[2]
    for z1 in range(2):
        total = got[2 * z1].astype(jnp.float32) + got[2 * z1 + 1].astype(jnp.float32)
        total = total.astype(out.dtype)
        for i in range(out.shape[0]):
            out[i, :, wide * z1 : wide * z1 + wide] = total


def sum_copies(got, out):
    total = got[0].astype(jnp.float32)
    for i in range(1, got.shape[0]):
        total += got[i].astype(jnp.float32)
    total = total.astype(out.dtype)
    for i in range(out.shape[0]):
        out[i] = total


def scale_copies(got, out_scale, in_scale, out):
    total = got[0].astype(jnp.float32)
    for i in range(1, got.shape[0]):
        total += got[i].astype(jnp.float32)
    total = (total / (out_scale[...] * in_scale[...] + DAMPING)).astype(out.dtype)
    for i in range(out.shape[0]):
        out[i] = total


def turn_in(grad, basis, out, left):
    count, _, wide = grad.shape
    q = wide // 4
    for y in range(count):
        for g in range(4):
            left[g, :, q * y : q * y + q] = grad[y, :, q * g : q * g + q]
    right = basis[...].reshape(count * q, basis.shape[2])
    for g in range(4):
        out[g] = dot(left[g], right, 1, 0).astype(out.dtype)


def turn_out(rows, own, other, out, left, right):
    q, wide = own.shape[1], rows.shape[3] // 2
    for x in range(4):
        for b in range(2):
            for h in range(2):
                left[2 * b + h, :, wide * x : wide * x + wide] = rows[
                    2 * x + b, 0, :, wide * h : wide * h + wide
                ]
    for i in range(8):
        right[2 * q * i : 2 * q * i + q] = own[i]
        right[2 * q * i + q : 2 * q * i + 2 * q] = other[i]
    right = right[...]
    for g in range(4):
        out[g] = dot(left[g], right, 1, 0).astype(out.dtype)


def back_in(scaled, basis, out):
    q = basis.shape[1]
    for y in range(basis.shape[0]):
        for g in range(4):
            out[y, :, q * g : q * g + q] = dot(scaled[g], basis[y], 1, 1).astype(out.dtype)


def back_out(part, rows, mine, other, keep, give, right):
    q, wide = mine.shape[0], mine.shape[1] // 2
    low = part[0] == 0
    for g in range(4):
        a = mine[:, wide // 2 * g : wide // 2 * (g + 1)]
        b = other[:, wide // 2 * g : wide // 2 * (g + 1)]
        right[g, :, : wide // 2] = jnp.where(low, a, b)
        right[g, :, wide // 2 :] = jnp.where(low, b, a)
    for x in range(4):
        for n in range(2):
            total = jnp.zeros((wide, wide), jnp.float32)
            for b in range(2):
                for h in range(2):
                    left = rows[2 * x + b, n, :, wide * h : wide * h + wide]
                    total += dot(left, right[2 * b + h], 0, 0)
            total = total.astype(keep.dtype)
            for z in range(2):
                at = 2 * q * z
                keep[2 * x + z, :, wide * n : wide * n + wide] = total[at : at + q]
                give[2 * x + z, :, wide * n : wide * n + wide] = total[at + q : at + 2 * q]


def body(grad_parts, basis_in, basis_out, eig_in, eig_out):
    bf16, f32 = jnp.bfloat16, jnp.float32
    x, z1, z0, c, y, z2 = (lax.axis_index(a) for a in AXES)
    rows, cols = basis_in.shape
    half, quarter = rows // 2, cols // 4
    wide = 2 * rows
    low_core, low_rep = c == 0, z2 == 0


    core, rep, part_z1 = (i.astype(jnp.int32).reshape(1) for i in (c, z2, z1))

    first = (((x * 2 + z1) * 2 + z0) * 2 + c) * rows + z2 * half
    out_scale = lax.dynamic_slice_in_dim(eig_out, first, half, 0)[:, None]
    in_scale = lax.dynamic_slice_in_dim(eig_in, y * cols, cols, 0)[None, :]

    bo = run(order_out, shape(2, half, cols), (core, rep, basis_out), flags=2)
    bo = lax.ppermute(bo, ("z1", "y"), pairs_z1y0())

    bi = basis_in.astype(bf16)
    bi = jnp.where(low_rep, bi[:half], bi[half:])
    bi = lax.ppermute(bi, ("z1", "z0", "c", "z2"), pairs_rows())

    grad = run(cut_grad, shape(4, half, wide), (grad_parts[0],))
    grad = lax.all_to_all(grad, PART, 0, 0, tiled=True)
    grad = run(join_grad, shape(8, half, cols), (grad,))

    bo, bi, grad = lax.optimization_barrier((bo, bi, grad))
    bi = gather(bi, RING, 8)
    bi = in_order(low_core, bi, lax.ppermute(bi, "c", SWAP), 1)
    grad = lax.all_to_all(grad, "y", 0, 0, tiled=True)

    bo, grad = lax.optimization_barrier((bo, grad))
    bo = lax.all_gather(bo, "y", axis=0)

    left = (4, half, 8 * quarter)
    part = run(turn_in, shape(4, half, cols), (grad, bi), (left,))
    part = lax.all_to_all(part, PART, 0, 0, tiled=True)
    turned = run(sum_copies, shape(8, half, cols), (part,))
    turned = lax.all_to_all(turned, RING, 0, 0, tiled=True)
    other = lax.ppermute(turned, "c", SWAP)

    right = (8 * rows, cols)
    part = run(turn_out, shape(4, half, cols), (bo, turned, other), (left, right))
    part = lax.all_to_all(part, PART, 0, 0, tiled=True)
    scaled = run(scale_copies, shape(4, half, cols), (part, out_scale, in_scale))
    scaled = lax.all_to_all(scaled, PART, 0, 0, tiled=True)

    part = run(back_in, shape(8, half, cols), (scaled, bi))
    back = scatter_sum(part, "y").astype(bf16)
    other = lax.ppermute(back, "z1", SWAP)

    keep, give = run(
        back_out,
        (shape(8, half, cols), shape(8, half, cols)),
        (part_z1, bo, back, other),
        ((4, half, wide),),
        flags=1,
    )
    part = (keep.astype(f32) + lax.ppermute(give, "c", SWAP).astype(f32)).astype(bf16)
    out = scatter_sum(part, RING).astype(bf16)
    return in_order(low_rep, out[:, :wide], out[:, wide:], 0)


def solution(mesh):
    fine = Mesh(mesh.devices.reshape(4, 2, 2, 2, 8, 2), AXES)
    in_specs = (P("z2", ROWS, "y"), P(ROWS, "y"), P(ROWS, "y"), P(), P())
    out_specs = P(ROWS, ("y", "z2"))
    return jax.shard_map(body, mesh=fine, in_specs=in_specs, out_specs=out_specs, check_vma=False)
```

```python
import jax
import jax.numpy as jnp
from jax import lax
from jax.experimental import pallas as pl
from jax.experimental.pallas import tpu as pltpu
from jax.sharding import Mesh, PartitionSpec as P

DAMPING = 0.1
AXES = ("x", "z1", "z0", "c", "y", "z2")
ROWS = ("x", "z1", "z0", "c")
RING = ("x", "z0")
PART = ("z1", "z2")
SWAP = [(0, 1), (1, 0)]


def gather(block, axes, count):
    return lax.all_to_all(
        jnp.broadcast_to(block[None], (count,) + block.shape), axes, 0, 0, tiled=True
    )


def scatter_sum(blocks, axes):
    got = lax.all_to_all(blocks, axes, 0, 0, tiled=True)
    return jnp.sum(got.astype(jnp.float32), axis=0)


def dot(left, right, left_dim, right_dim):
    return lax.dot_general(
        left, right, (((left_dim,), (right_dim,)), ((), ())), preferred_element_type=jnp.float32
    )


def in_order(first, mine, other, axis):
    return jnp.where(
        first,
        jnp.concatenate([mine, other], axis=axis),
        jnp.concatenate([other, mine], axis=axis),
    )


def pairs_z1y0():
    return [(z1 * 8 + y, (y % 2) * 8 + (y // 2) * 2 + z1) for z1 in range(2) for y in range(8)]


def pairs_rows():
    return [
        (z1 * 8 + z0 * 4 + c * 2 + z2, c * 8 + z1 * 4 + z2 * 2 + z0)
        for z1 in range(2)
        for z0 in range(2)
        for c in range(2)
        for z2 in range(2)
    ]


def run(kernel, outs, args, scratch=(), flags=0):
    size = sum(a.size * a.dtype.itemsize for a in (*args, *jax.tree.leaves(outs)))
    return pl.pallas_call(
        kernel,
        out_shape=outs,
        in_specs=[
            pl.BlockSpec(memory_space=pltpu.SMEM if i < flags else pltpu.VMEM)
            for i in range(len(args))
        ],
        scratch_shapes=[pltpu.VMEM(shape, jnp.bfloat16) for shape in scratch],
        cost_estimate=pl.CostEstimate(flops=2 * 288 * 1152 * 576, bytes_accessed=size, transcendentals=0),
        compiler_params=pltpu.CompilerParams(vmem_limit_bytes=32 * 2**20),
    )(*args)


def shape(*dims):
    return jax.ShapeDtypeStruct(dims, jnp.bfloat16)


def order_out(core, rep, rows, out):
    q = out.shape[1]
    low_core, low_rep = core[0] == 0, rep[0] == 0
    for a in range(2):
        block = rows[q * a : q * a + q].astype(jnp.bfloat16).astype(jnp.float32)
        for t in range(4):
            def cut(block_c, half):
                at = (4 * (t // 2) + 2 * block_c + half) * q
                return block[:, at : at + q]

            for far in range(2):
                first = jnp.where(low_core, cut(t % 2, far), cut(1 - t % 2, far))
                second = jnp.where(low_core, cut(t % 2, 1 - far), cut(1 - t % 2, 1 - far))
                at = (4 * a + t) * q
                out[far, :, at : at + q] = jnp.where(low_rep, first, second).astype(jnp.bfloat16)


def cut_grad(grad, out):
    q, wide = grad.shape[0] // 2, grad.shape[1] // 4
    for part, block in enumerate((0, 2, 1, 3)):
        for h in range(2):
            piece = grad[q * h : q * h + q, wide * block : wide * block + wide]
            out[part, :, wide * h : wide * h + wide] = piece


def join_grad(got, out):
    wide = got.shape[2]
    for z1 in range(2):
        total = got[2 * z1].astype(jnp.float32) + got[2 * z1 + 1].astype(jnp.float32)
        total = total.astype(out.dtype)
        for i in range(out.shape[0]):
            out[i, :, wide * z1 : wide * z1 + wide] = total


def sum_copies(p0, p1, p2, p3, out):
    total = p0[...].astype(jnp.float32)
    for p in (p1, p2, p3):
        total += p[...].astype(jnp.float32)
    total = total.astype(out.dtype)
    for i in range(out.shape[0]):
        out[i] = total


def scale(got, out_scale, in_scale, out):
    total = got[0].astype(jnp.float32)
    for i in range(1, got.shape[0]):
        total += got[i].astype(jnp.float32)
    total = (total / (out_scale[...] * in_scale[...] + DAMPING)).astype(out.dtype)
    for i in range(out.shape[0]):
        out[i] = total


def join_out(rep, got, out):
    total = got[0].astype(jnp.float32)
    for i in range(1, got.shape[0]):
        total += got[i].astype(jnp.float32)
    total = total.astype(out.dtype)
    q, wide = out.shape[0] // 2, out.shape[1]
    low = rep[0] == 0
    near, far = total[:, :wide], total[:, wide:]
    out[:q] = jnp.where(low, near, far)
    out[q:] = jnp.where(low, far, near)


def to_part(block, d):
    return lax.ppermute(block, PART, [(i, i ^ d) for i in range(4)])


def turn_in(part, grad, basis, *outs_and_left):
    *outs, left = outs_and_left
    count, _, wide = grad.shape
    q = wide // 4
    for y in range(count):
        for g in range(4):
            left[g, :, q * y : q * y + q] = grad[y, :, q * g : q * g + q]
    right = basis[...].reshape(count * q, basis.shape[2])
    for d, out in enumerate(outs):
        out[...] = dot(left[part[0] ^ d], right, 1, 0).astype(out.dtype)


def turn_out(rows, own, other, out, left, right):
    q, wide = own.shape[1], rows.shape[3] // 2
    for x in range(4):
        for b in range(2):
            for h in range(2):
                left[2 * b + h, :, wide * x : wide * x + wide] = rows[
                    2 * x + b, 0, :, wide * h : wide * h + wide
                ]
    for i in range(8):
        right[2 * q * i : 2 * q * i + q] = own[i]
        right[2 * q * i + q : 2 * q * i + 2 * q] = other[i]
    right = right[...]
    for g in range(4):
        out[g] = dot(left[g], right, 1, 0).astype(out.dtype)


def back_in(scaled, basis, out):
    q = basis.shape[1]
    for y in range(basis.shape[0]):
        for g in range(4):
            out[y, :, q * g : q * g + q] = dot(scaled[g], basis[y], 1, 1).astype(out.dtype)


def back_out(part, rows, mine, other, keep, give, right):
    q, wide = mine.shape[0], mine.shape[1] // 2
    low = part[0] == 0
    for g in range(4):
        a = mine[:, wide // 2 * g : wide // 2 * (g + 1)]
        b = other[:, wide // 2 * g : wide // 2 * (g + 1)]
        right[g, :, : wide // 2] = jnp.where(low, a, b)
        right[g, :, wide // 2 :] = jnp.where(low, b, a)
    for x in range(4):
        for n in range(2):
            total = jnp.zeros((wide, wide), jnp.float32)
            for b in range(2):
                for h in range(2):
                    left = rows[2 * x + b, n, :, wide * h : wide * h + wide]
                    total += dot(left, right[2 * b + h], 0, 0)
            total = total.astype(keep.dtype)
            for z in range(2):
                at = 2 * q * z
                keep[2 * x + z, :, wide * n : wide * n + wide] = total[at : at + q]
                give[2 * x + z, :, wide * n : wide * n + wide] = total[at + q : at + 2 * q]


def body(grad_parts, basis_in, basis_out, eig_in, eig_out):
    bf16, f32 = jnp.bfloat16, jnp.float32
    x, z1, z0, c, y, z2 = (lax.axis_index(a) for a in AXES)
    rows, cols = basis_in.shape
    half, quarter = rows // 2, cols // 4
    wide = 2 * rows
    low_core, low_rep = c == 0, z2 == 0


    core, rep, part_z1, this_part = (
        i.astype(jnp.int32).reshape(1) for i in (c, z2, z1, 2 * z1 + z2)
    )

    first = (((x * 2 + z1) * 2 + z0) * 2 + c) * rows + z2 * half
    out_scale = lax.dynamic_slice_in_dim(eig_out, first, half, 0)[:, None]
    in_scale = lax.dynamic_slice_in_dim(eig_in, y * cols, cols, 0)[None, :]

    bo = run(order_out, shape(2, half, cols), (core, rep, basis_out), flags=2)
    bo = lax.ppermute(bo, ("z1", "y"), pairs_z1y0())

    bi = basis_in.astype(bf16)
    bi = jnp.where(low_rep, bi[:half], bi[half:])
    bi = lax.ppermute(bi, ("z1", "z0", "c", "z2"), pairs_rows())

    grad = run(cut_grad, shape(4, half, wide), (grad_parts[0],))
    grad = lax.all_to_all(grad, PART, 0, 0, tiled=True)
    grad = run(join_grad, shape(8, half, cols), (grad,))

    bo, bi, grad = lax.optimization_barrier((bo, bi, grad))
    bi = gather(bi, RING, 8)
    bi = in_order(low_core, bi, lax.ppermute(bi, "c", SWAP), 1)
    grad = lax.all_to_all(grad, "y", 0, 0, tiled=True)

    bo, grad = lax.optimization_barrier((bo, grad))
    bo = lax.all_gather(bo, "y", axis=0)

    left = (4, half, 8 * quarter)
    blocks = run(turn_in, (shape(half, cols),) * 4, (this_part, grad, bi), (left,), 1)
    blocks = [blocks[0]] + [to_part(blocks[d], d) for d in (1, 2, 3)]
    turned = run(sum_copies, shape(8, half, cols), blocks)
    turned = lax.all_to_all(turned, RING, 0, 0, tiled=True)
    other = lax.ppermute(turned, "c", SWAP)

    right = (8 * rows, cols)
    part = run(turn_out, shape(4, half, cols), (bo, turned, other), (left, right))
    part = lax.all_to_all(part, PART, 0, 0, tiled=True)
    scaled = run(scale, shape(4, half, cols), (part, out_scale, in_scale))
    scaled = lax.all_to_all(scaled, PART, 0, 0, tiled=True)

    part = run(back_in, shape(8, half, cols), (scaled, bi))
    back = scatter_sum(part, "y").astype(bf16)
    other = lax.ppermute(back, "z1", SWAP)

    keep, give = run(
        back_out,
        (shape(8, half, cols), shape(8, half, cols)),
        (part_z1, bo, back, other),
        ((4, half, wide),),
        flags=1,
    )
    part = (keep.astype(f32) + lax.ppermute(give, "c", SWAP).astype(f32)).astype(bf16)
    part = lax.all_to_all(part, RING, 0, 0, tiled=True)
    return run(join_out, shape(rows, wide), (rep, part), flags=1)


def solution(mesh):
    fine = Mesh(mesh.devices.reshape(4, 2, 2, 2, 8, 2), AXES)
    in_specs = (P("z2", ROWS, "y"), P(ROWS, "y"), P(ROWS, "y"), P(), P())
    out_specs = P(ROWS, ("y", "z2"))
    return jax.shard_map(body, mesh=fine, in_specs=in_specs, out_specs=out_specs, check_vma=False)
```

```python
import jax
import jax.numpy as jnp
from jax import lax
from jax.experimental import pallas as pl
from jax.experimental.pallas import tpu as pltpu
from jax.sharding import Mesh, PartitionSpec as P

DAMPING = 0.1
AXES = ("x", "z1", "z0", "c", "y", "z2")
ROWS = ("x", "z1", "z0", "c")
RING = ("x", "z0")
PART = ("z1", "z2")
SWAP = [(0, 1), (1, 0)]


def scatter_sum(blocks, axes):
    got = lax.all_to_all(blocks, axes, 0, 0, tiled=True)
    return jnp.sum(got.astype(jnp.float32), axis=0)


def dot(left, right, left_dim, right_dim):
    return lax.dot_general(
        left, right, (((left_dim,), (right_dim,)), ((), ())), preferred_element_type=jnp.float32
    )


def pairs_z1y0():
    return [(z1 * 8 + y, (y % 2) * 8 + (y // 2) * 2 + z1) for z1 in range(2) for y in range(8)]


def pairs_rows():
    return [
        (z1 * 8 + z0 * 4 + c * 2 + z2, c * 8 + z1 * 4 + z2 * 2 + z0)
        for z1 in range(2)
        for z0 in range(2)
        for c in range(2)
        for z2 in range(2)
    ]


def run(kernel, outs, args, scratch=(), flags=0):
    size = sum(a.size * a.dtype.itemsize for a in (*args, *jax.tree.leaves(outs)))
    return pl.pallas_call(
        kernel,
        out_shape=outs,
        in_specs=[
            pl.BlockSpec(memory_space=pltpu.SMEM if i < flags else pltpu.VMEM)
            for i in range(len(args))
        ],
        scratch_shapes=[pltpu.VMEM(shape, jnp.bfloat16) for shape in scratch],
        cost_estimate=pl.CostEstimate(flops=2 * 288 * 1152 * 576, bytes_accessed=size, transcendentals=0),
        compiler_params=pltpu.CompilerParams(vmem_limit_bytes=32 * 2**20),
    )(*args)


def shape(*dims):
    return jax.ShapeDtypeStruct(dims, jnp.bfloat16)


def order_out(core, rep, rows, out):
    q = out.shape[1]
    low_core, low_rep = core[0] == 0, rep[0] == 0
    for a in range(2):
        block = rows[q * a : q * a + q].astype(jnp.bfloat16).astype(jnp.float32)
        for t in range(4):
            def cut(block_c, half):
                at = (4 * (t // 2) + 2 * block_c + half) * q
                return block[:, at : at + q]

            for far in range(2):
                first = jnp.where(low_core, cut(t % 2, far), cut(1 - t % 2, far))
                second = jnp.where(low_core, cut(t % 2, 1 - far), cut(1 - t % 2, 1 - far))
                at = (4 * a + t) * q
                out[far, :, at : at + q] = jnp.where(low_rep, first, second).astype(jnp.bfloat16)


def cut_grad(grad, out):
    q, wide = grad.shape[0] // 2, grad.shape[1] // 4
    for part, block in enumerate((0, 2, 1, 3)):
        for h in range(2):
            piece = grad[q * h : q * h + q, wide * block : wide * block + wide]
            out[part, :, wide * h : wide * h + wide] = piece


def join_grad(got, out):
    wide = got.shape[2]
    for z1 in range(2):
        total = got[2 * z1].astype(jnp.float32) + got[2 * z1 + 1].astype(jnp.float32)
        total = total.astype(out.dtype)
        for i in range(out.shape[0]):
            out[i, :, wide * z1 : wide * z1 + wide] = total


def sum_copies(p0, p1, p2, p3, out):
    total = p0[...].astype(jnp.float32)
    for p in (p1, p2, p3):
        total += p[...].astype(jnp.float32)
    total = total.astype(out.dtype)
    for i in range(out.shape[0]):
        out[i] = total


def scale(got, out_scale, in_scale, out):
    total = got[0].astype(jnp.float32)
    for i in range(1, got.shape[0]):
        total += got[i].astype(jnp.float32)
    total = (total / (out_scale[...] * in_scale[...] + DAMPING)).astype(out.dtype)
    for i in range(out.shape[0]):
        out[i] = total


def join_out(rep, got, out):
    total = got[0].astype(jnp.float32)
    for i in range(1, got.shape[0]):
        total += got[i].astype(jnp.float32)
    total = total.astype(out.dtype)
    q, wide = out.shape[0] // 2, out.shape[1]
    low = rep[0] == 0
    near, far = total[:, :wide], total[:, wide:]
    out[:q] = jnp.where(low, near, far)
    out[q:] = jnp.where(low, far, near)


def to_part(block, d):
    return lax.ppermute(block, PART, [(i, i ^ d) for i in range(4)])


def turn_in(part, grad, basis, *outs_and_left):
    *outs, left = outs_and_left
    count, _, wide = grad.shape
    q = wide // 4
    for y in range(count):
        for g in range(4):
            left[g, :, q * y : q * y + q] = grad[y, :, q * g : q * g + q]
    right = basis[...].reshape(count * q, basis.shape[2])
    for d, out in enumerate(outs):
        out[...] = dot(left[part[0] ^ d], right, 1, 0).astype(out.dtype)


def turn_out(rows, own, other, out, left, right):
    q, wide = own.shape[1], rows.shape[3] // 2
    for x in range(4):
        for b in range(2):
            for h in range(2):
                left[2 * b + h, :, wide * x : wide * x + wide] = rows[
                    2 * x + b, 0, :, wide * h : wide * h + wide
                ]
    for i in range(8):
        right[2 * q * i : 2 * q * i + q] = own[i]
        right[2 * q * i + q : 2 * q * i + 2 * q] = other[i]
    right = right[...]
    for g in range(4):
        out[g] = dot(left[g], right, 1, 0).astype(out.dtype)


def back_in(scaled, basis, out):
    q = basis.shape[1]
    for y in range(basis.shape[0]):
        for g in range(4):
            out[y, :, q * g : q * g + q] = dot(scaled[g], basis[y], 1, 1).astype(out.dtype)


def back_out(part, rows, mine, other, keep, give, right):
    q, wide = mine.shape[0], mine.shape[1] // 2
    low = part[0] == 0
    for g in range(4):
        a = mine[:, wide // 2 * g : wide // 2 * (g + 1)]
        b = other[:, wide // 2 * g : wide // 2 * (g + 1)]
        right[g, :, : wide // 2] = jnp.where(low, a, b)
        right[g, :, wide // 2 :] = jnp.where(low, b, a)
    for x in range(4):
        for n in range(2):
            total = jnp.zeros((wide, wide), jnp.float32)
            for b in range(2):
                for h in range(2):
                    left = rows[2 * x + b, n, :, wide * h : wide * h + wide]
                    total += dot(left, right[2 * b + h], 0, 0)
            total = total.astype(keep.dtype)
            for z in range(2):
                at = 2 * q * z
                keep[2 * x + z, :, wide * n : wide * n + wide] = total[at : at + q]
                give[2 * x + z, :, wide * n : wide * n + wide] = total[at + q : at + 2 * q]


def body(grad_parts, basis_in, basis_out, eig_in, eig_out):
    bf16, f32 = jnp.bfloat16, jnp.float32
    x, z1, z0, c, y, z2 = (lax.axis_index(a) for a in AXES)
    rows, cols = basis_in.shape
    half, quarter = rows // 2, cols // 4
    wide = 2 * rows


    core, rep, part_z1, this_part = (
        i.astype(jnp.int32).reshape(1) for i in (c, z2, z1, 2 * z1 + z2)
    )

    first = (((x * 2 + z1) * 2 + z0) * 2 + c) * rows + z2 * half
    out_scale = lax.dynamic_slice_in_dim(eig_out, first, half, 0)[:, None]
    in_scale = lax.dynamic_slice_in_dim(eig_in, y * cols, cols, 0)[None, :]

    bi = basis_in.astype(bf16)
    bi = lax.ppermute(bi, ("z1", "z0", "c", "z2"), pairs_rows())
    bi, grad_parts = lax.optimization_barrier((bi, grad_parts))
    bi = lax.all_gather(bi, RING, axis=0)

    bo = run(order_out, shape(2, half, cols), (core, rep, basis_out), flags=2)
    bo = lax.ppermute(bo, ("z1", "y"), pairs_z1y0())

    grad = run(cut_grad, shape(4, half, wide), (grad_parts[0],))
    grad = lax.all_to_all(grad, PART, 0, 0, tiled=True)
    grad = run(join_grad, shape(8, half, cols), (grad,))

    bo, grad = lax.optimization_barrier((bo, grad))
    grad = lax.all_to_all(grad, "y", 0, 0, tiled=True)

    bo, grad = lax.optimization_barrier((bo, grad))
    bo = lax.all_gather(bo, "y", axis=0)

    left = (4, half, 8 * quarter)
    blocks = run(turn_in, (shape(half, cols),) * 4, (this_part, grad, bi), (left,), 1)
    blocks = [blocks[0]] + [to_part(blocks[d], d) for d in (1, 2, 3)]
    turned = run(sum_copies, shape(8, half, cols), blocks)
    turned = lax.all_to_all(turned, RING, 0, 0, tiled=True)
    other = lax.ppermute(turned, "c", SWAP)

    right = (8 * rows, cols)
    part = run(turn_out, shape(4, half, cols), (bo, turned, other), (left, right))
    part = lax.all_to_all(part, PART, 0, 0, tiled=True)
    scaled = run(scale, shape(4, half, cols), (part, out_scale, in_scale))
    scaled = lax.all_to_all(scaled, PART, 0, 0, tiled=True)

    part = run(back_in, shape(8, half, cols), (scaled, bi))
    back = scatter_sum(part, "y").astype(bf16)
    other = lax.ppermute(back, "z1", SWAP)

    keep, give = run(
        back_out,
        (shape(8, half, cols), shape(8, half, cols)),
        (part_z1, bo, back, other),
        ((4, half, wide),),
        flags=1,
    )
    part = (keep.astype(f32) + lax.ppermute(give, "c", SWAP).astype(f32)).astype(bf16)
    part = lax.all_to_all(part, RING, 0, 0, tiled=True)
    return run(join_out, shape(rows, wide), (rep, part), flags=1)


def solution(mesh):
    fine = Mesh(mesh.devices.reshape(4, 2, 2, 2, 8, 2), AXES)
    in_specs = (P("z2", ROWS, "y"), P(ROWS, "y"), P(ROWS, "y"), P(), P())
    out_specs = P(ROWS, ("y", "z2"))
    return jax.shard_map(body, mesh=fine, in_specs=in_specs, out_specs=out_specs, check_vma=False)
```

```python
import functools

import jax
import jax.numpy as jnp
from jax import lax
from jax.experimental import pallas as pl
from jax.experimental.pallas import tpu as pltpu
from jax.sharding import Mesh, PartitionSpec as P

DAMPING = 0.1
AXES = ("x", "z1", "z0", "c", "y", "z2")
ROWS = ("x", "z1", "z0", "c")
RING = ("x", "z0")
PART = ("z1", "z2")
SWAP = [(0, 1), (1, 0)]


def scatter_sum(blocks, axes):
    got = lax.all_to_all(blocks, axes, 0, 0, tiled=True)
    return jnp.sum(got.astype(jnp.float32), axis=0)


def dot(left, right, left_dim, right_dim):
    return lax.dot_general(
        left, right, (((left_dim,), (right_dim,)), ((), ())), preferred_element_type=jnp.float32
    )


def pairs_z1y0():
    return [(z1 * 8 + y, (y % 2) * 8 + (y // 2) * 2 + z1) for z1 in range(2) for y in range(8)]


def pairs_rows():
    return [
        (z1 * 8 + z0 * 4 + c * 2 + z2, c * 8 + z1 * 4 + z2 * 2 + z0)
        for z1 in range(2)
        for z0 in range(2)
        for c in range(2)
        for z2 in range(2)
    ]


def run(kernel, outs, args, scratch=(), flags=0):
    size = sum(a.size * a.dtype.itemsize for a in (*args, *jax.tree.leaves(outs)))
    return pl.pallas_call(
        kernel,
        out_shape=outs,
        in_specs=[
            pl.BlockSpec(memory_space=pltpu.SMEM if i < flags else pltpu.VMEM)
            for i in range(len(args))
        ],
        scratch_shapes=[pltpu.VMEM(shape, jnp.bfloat16) for shape in scratch],
        cost_estimate=pl.CostEstimate(flops=2 * 288 * 1152 * 576, bytes_accessed=size, transcendentals=0),
        compiler_params=pltpu.CompilerParams(vmem_limit_bytes=32 * 2**20),
    )(*args)


def shape(*dims):
    return jax.ShapeDtypeStruct(dims, jnp.bfloat16)


def order_out(core, rep, rows, out):
    q = out.shape[1]
    low_core, low_rep = core[0] == 0, rep[0] == 0
    for a in range(2):
        block = rows[q * a : q * a + q].astype(jnp.bfloat16).astype(jnp.float32)
        for t in range(4):
            def cut(block_c, half):
                at = (4 * (t // 2) + 2 * block_c + half) * q
                return block[:, at : at + q]

            for far in range(2):
                first = jnp.where(low_core, cut(t % 2, far), cut(1 - t % 2, far))
                second = jnp.where(low_core, cut(t % 2, 1 - far), cut(1 - t % 2, 1 - far))
                at = (4 * a + t) * q
                out[far, :, at : at + q] = jnp.where(low_rep, first, second).astype(jnp.bfloat16)


def cut_grad(grad, out):
    q, wide = grad.shape[0] // 2, grad.shape[1] // 4
    for part, block in enumerate((0, 2, 1, 3)):
        for h in range(2):
            piece = grad[q * h : q * h + q, wide * block : wide * block + wide]
            out[part, :, wide * h : wide * h + wide] = piece


def join_grad(got, out):
    wide = got.shape[2]
    for z1 in range(2):
        total = got[2 * z1].astype(jnp.float32) + got[2 * z1 + 1].astype(jnp.float32)
        total = total.astype(out.dtype)
        for i in range(out.shape[0]):
            out[i, :, wide * z1 : wide * z1 + wide] = total


def sum_copies(p0, p1, p2, p3, out):
    total = p0[...].astype(jnp.float32)
    for p in (p1, p2, p3):
        total += p[...].astype(jnp.float32)
    total = total.astype(out.dtype)
    for i in range(out.shape[0]):
        out[i] = total


def scale(got, out_scale, in_scale, out):
    total = got[0].astype(jnp.float32)
    for i in range(1, got.shape[0]):
        total += got[i].astype(jnp.float32)
    total = (total / (out_scale[...] * in_scale[...] + DAMPING)).astype(out.dtype)
    for i in range(out.shape[0]):
        out[i] = total


def join_out(rep, got, out):
    total = got[0].astype(jnp.float32)
    for i in range(1, got.shape[0]):
        total += got[i].astype(jnp.float32)
    total = total.astype(out.dtype)
    q, wide = out.shape[0] // 2, out.shape[1]
    low = rep[0] == 0
    near, far = total[:, :wide], total[:, wide:]
    out[:q] = jnp.where(low, near, far)
    out[q:] = jnp.where(low, far, near)


def to_part(block, d):
    return lax.ppermute(block, PART, [(i, i ^ d) for i in range(4)])


def turn_in(part, grad, basis, *outs_and_left):
    *outs, left = outs_and_left
    count, _, wide = grad.shape
    q = wide // 4
    for y in range(count):
        for g in range(4):
            left[g, :, q * y : q * y + q] = grad[y, :, q * g : q * g + q]
    right = basis[...].reshape(count * q, basis.shape[2])
    for d, out in enumerate(outs):
        out[...] = dot(left[part[0] ^ d], right, 1, 0).astype(out.dtype)


def turn_out(rows, own, other, out, left, right):
    q, wide = own.shape[1], rows.shape[3] // 2
    for x in range(4):
        for b in range(2):
            for h in range(2):
                left[2 * b + h, :, wide * x : wide * x + wide] = rows[
                    2 * x + b, 0, :, wide * h : wide * h + wide
                ]
    for i in range(8):
        right[2 * q * i : 2 * q * i + q] = own[i]
        right[2 * q * i + q : 2 * q * i + 2 * q] = other[i]
    right = right[...]
    for g in range(4):
        out[g] = dot(left[g], right, 1, 0).astype(out.dtype)


def back_in(scaled, basis, out):
    q = basis.shape[1]
    for y in range(basis.shape[0]):
        for g in range(4):
            out[y, :, q * g : q * g + q] = dot(scaled[g], basis[y], 1, 1).astype(out.dtype)


def back_out(side, part, rows, mine, other, out, right):
    q, wide = mine.shape[0], mine.shape[1] // 2
    low = part[0] == 0
    for g in range(4):
        a = mine[:, wide // 2 * g : wide // 2 * (g + 1)]
        b = other[:, wide // 2 * g : wide // 2 * (g + 1)]
        right[g, :, : wide // 2] = jnp.where(low, a, b)
        right[g, :, wide // 2 :] = jnp.where(low, b, a)
    for x in range(4):
        for n in range(2):
            total = jnp.zeros((2 * q, wide), jnp.float32)
            for b in range(2):
                for h in range(2):
                    at = wide * h + q * side
                    left = jnp.concatenate(
                        [
                            rows[2 * x + b, n, :, at : at + q],
                            rows[2 * x + b, n, :, at + 2 * q : at + 3 * q],
                        ],
                        axis=1,
                    )
                    total += dot(left, right[2 * b + h], 0, 0)
            total = total.astype(out.dtype)
            for z in range(2):
                out[2 * x + z, :, wide * n : wide * n + wide] = total[q * z : q * z + q]


def body(grad_parts, basis_in, basis_out, eig_in, eig_out):
    bf16, f32 = jnp.bfloat16, jnp.float32
    x, z1, z0, c, y, z2 = (lax.axis_index(a) for a in AXES)
    rows, cols = basis_in.shape
    half, quarter = rows // 2, cols // 4
    wide = 2 * rows


    core, rep, part_z1, this_part = (
        i.astype(jnp.int32).reshape(1) for i in (c, z2, z1, 2 * z1 + z2)
    )

    first = (((x * 2 + z1) * 2 + z0) * 2 + c) * rows + z2 * half
    out_scale = lax.dynamic_slice_in_dim(eig_out, first, half, 0)[:, None]
    in_scale = lax.dynamic_slice_in_dim(eig_in, y * cols, cols, 0)[None, :]

    bi = basis_in.astype(bf16)
    bi = lax.ppermute(bi, ("z1", "z0", "c", "z2"), pairs_rows())
    bi, grad_parts = lax.optimization_barrier((bi, grad_parts))
    bi = lax.all_gather(bi, RING, axis=0)

    bo = run(order_out, shape(2, half, cols), (core, rep, basis_out), flags=2)
    bo = lax.ppermute(bo, ("z1", "y"), pairs_z1y0())

    grad = run(cut_grad, shape(4, half, wide), (grad_parts[0],))
    grad = lax.all_to_all(grad, PART, 0, 0, tiled=True)
    grad = run(join_grad, shape(8, half, cols), (grad,))

    bo, grad = lax.optimization_barrier((bo, grad))
    grad = lax.all_to_all(grad, "y", 0, 0, tiled=True)

    bo, grad = lax.optimization_barrier((bo, grad))
    bo = lax.all_gather(bo, "y", axis=0)

    left = (4, half, 8 * quarter)
    blocks = run(turn_in, (shape(half, cols),) * 4, (this_part, grad, bi), (left,), 1)
    blocks = [blocks[0]] + [to_part(blocks[d], d) for d in (1, 2, 3)]
    turned = run(sum_copies, shape(8, half, cols), blocks)
    turned = lax.all_to_all(turned, RING, 0, 0, tiled=True)
    other = lax.ppermute(turned, "c", SWAP)

    right = (8 * rows, cols)
    part = run(turn_out, shape(4, half, cols), (bo, turned, other), (left, right))
    part = lax.all_to_all(part, PART, 0, 0, tiled=True)
    scaled = run(scale, shape(4, half, cols), (part, out_scale, in_scale))
    scaled = lax.all_to_all(scaled, PART, 0, 0, tiled=True)

    part = run(back_in, shape(8, half, cols), (scaled, bi))
    back = scatter_sum(part, "y").astype(bf16)
    other = lax.ppermute(back, "z1", SWAP)

    def half_of_m(side):
        return run(
            functools.partial(back_out, side),
            shape(8, half, cols),
            (part_z1, bo, back, other),
            ((4, half, wide),),
            flags=1,
        )

    got = lax.ppermute(half_of_m(1), "c", SWAP)
    part = (half_of_m(0).astype(f32) + got.astype(f32)).astype(bf16)
    part = lax.all_to_all(part, RING, 0, 0, tiled=True)
    return run(join_out, shape(rows, wide), (rep, part), flags=1)


def solution(mesh):
    fine = Mesh(mesh.devices.reshape(4, 2, 2, 2, 8, 2), AXES)
    in_specs = (P("z2", ROWS, "y"), P(ROWS, "y"), P(ROWS, "y"), P(), P())
    out_specs = P(ROWS, ("y", "z2"))
    return jax.shard_map(body, mesh=fine, in_specs=in_specs, out_specs=out_specs, check_vma=False)
```
